32 devices in a mesh: row: 8 (over y, x, core), col: 4 (over z).
Axes of the slice: x: 2, y: 2, z: 4, core: 2. Of those that a mesh axis runs over, the one named last changes fastest.
Arguments:
- gram_panel: float32 [2048, 1024], P('row', 'col'), may hold values from -1495.4 to 1495.4, as said below
- left_factor: bfloat16 [2048, 4096], P('row', 'col'), may hold values from -0.6 to 0.6
- solved_prev: bfloat16 [4096, 2048], P('row', 'col'), may hold values from -0.59765625 to 0.59765625
- right_block: float32 [1024, 2048], P('row', 'col'), may hold values from -6 to 6
Outputs:
- panel_factor: float32 [2048, 1024], P('row', 'col')
- solved_panel: float32 [1024, 2048], P('row', 'col')
The draws below stay inside these ranges and needn't reach their ends.
Inputs may be any that keep to these rules, and one draw needn't show every extreme that they name: The rows of gram_panel at the panel's indices minus the product of the corresponding rows of left_factor with their transpose form a symmetric positive definite matrix.
All inputs are finite; a program needn't handle non-finite values.
Results may differ from the reference program's by a relative error of at most 0.0006.
Values may be sent and summed in bfloat16 or wider, within the bound.
A program may use at most 64 MiB of HBM per device.

```python
import jax
import jax.numpy as jnp
from jax import lax

PANEL = 1024
ROWS_DEV = 256
ROWS = 2048
PREV = 4096
VOX = 2048
BLOCK = 128
N_ROW = 8


def panel_index_drawn():
    grid = jnp.arange(N_ROW, dtype=jnp.int32)[:, None] * ROWS_DEV + jnp.arange(BLOCK, dtype=jnp.int32)[None, :]
    return grid.reshape(-1).astype(jnp.int32)


def left_values(key):
    source = jax.random.fold_in(key, 17)
    spread = 0.95 * PREV ** (-0.25)
    values = jnp.clip(jax.random.normal(source, (ROWS, PREV), jnp.float32), -5.0, 5.0) * spread
    return values.astype(jnp.bfloat16)


def draw_left_factor(key, part):
    return left_values(key)


def draw_gram_panel(key, part):
    left = left_values(key).astype(jnp.float32)
    chosen = left[panel_index_drawn()]
    cross = jnp.dot(chosen, chosen.T, precision=lax.Precision.HIGHEST)
    first = jax.random.fold_in(jax.random.fold_in(key, 29), 0)
    third = jax.random.fold_in(jax.random.fold_in(key, 29), 2)
    fourth = jax.random.fold_in(jax.random.fold_in(key, 29), 3)
    outer = jnp.clip(jax.random.normal(first, (ROWS, PANEL), jnp.float32), -6.0, 6.0) * 0.9
    basis = jnp.clip(jax.random.normal(third, (PANEL, PANEL), jnp.float32), -4.0, 4.0)
    mixed = jnp.dot(basis, basis.T, precision=lax.Precision.HIGHEST) / PANEL
    mixed = 0.5 * (mixed + mixed.T)
    ridge = jax.random.uniform(fourth, (PANEL,), jnp.float32, 0.1, 0.3)
    block = cross + mixed + jnp.diag(ridge)
    return outer.at[panel_index_drawn()].set(block)


def block_scale(own_key, extent, shards, least, top_value):
    def one(axis_at, blocks):
        steps = jax.random.uniform(jax.random.fold_in(jax.random.fold_in(own_key, 6), axis_at), (blocks,), jnp.float32, least / len(shards), top_value / len(shards))
        return jnp.repeat(jnp.exp(steps), extent[axis_at] // blocks).reshape((-1,) + (1,) * (len(extent) - axis_at - 1))

    loudness = one(*shards[0])
    for cut in shards[1:]:
        loudness = loudness * one(*cut)
    return loudness


def gaussian(rng, extent, scale, reach, pieces=(), held_as=jnp.bfloat16):
    array = jax.random.normal(rng, extent, jnp.float32) * scale
    if len(pieces) > 0:
        array = block_scale(rng, extent, pieces, -0.22, 0.18) * array
    return jnp.clip(array, min=-reach, max=reach).astype(held_as)


def setup_inputs(seed: int = 0) -> dict:
    seeds = jax.random.split(jax.random.key(seed), 5)
    gram_panel = draw_gram_panel(jax.random.fold_in(seeds[4], 71), 0)
    left_factor = draw_left_factor(jax.random.fold_in(seeds[4], 71), 0)
    solved_prev = gaussian(seeds[2], (PREV, VOX), 0.1, 0.59765625, ((0, 8), (1, 4)))
    right_block = gaussian(seeds[3], (PANEL, VOX), 1.0, 6.0, ((0, 8), (1, 4)), jnp.float32)
    return {"gram_panel": gram_panel, "left_factor": left_factor, "solved_prev": solved_prev, "right_block": right_block}


def panel_index():
    grid = jnp.arange(N_ROW, dtype=jnp.int32)[:, None] * ROWS_DEV + jnp.arange(BLOCK, dtype=jnp.int32)[None, :]
    return grid.reshape(-1).astype(jnp.int32)

def reference(gram_panel, left_factor, solved_prev, right_block):
    chosen = left_factor[panel_index()]
    update = gram_panel - jnp.dot(left_factor.astype(jnp.float32), chosen.T.astype(jnp.float32), preferred_element_type=jnp.float32)
    diagonal = update[panel_index()]
    factor = jnp.linalg.cholesky(diagonal)
    inverse = jax.scipy.linalg.solve_triangular(factor, jnp.eye(PANEL, dtype=jnp.float32), lower=True)
    panel_factor = jnp.dot(update, inverse.T, precision=lax.Precision.HIGHEST)
    reduced = right_block - jnp.dot(chosen.astype(jnp.float32), solved_prev.astype(jnp.float32), preferred_element_type=jnp.float32)
    solved_panel = jnp.dot(inverse, reduced, precision=lax.Precision.HIGHEST)
    return (panel_factor, solved_panel)
```

```python
import functools

import jax
import jax.numpy as jnp
from jax import lax
from jax.experimental import pallas as pl
from jax.experimental.pallas import tpu as pltpu
from jax.sharding import PartitionSpec as P

STRIP = 8
TILE = 128


def halves(value):
    high = value.astype(jnp.bfloat16)
    low = (value - high.astype(jnp.float32)).astype(jnp.bfloat16)
    return high, low


def dot3(left, right, dims=((1,), (0,))):
    lh, ll = halves(left)
    rh, rl = halves(right)
    a = jnp.concatenate([lh, lh, ll], axis=dims[0][0])
    b = jnp.concatenate([rh, rl, rh], axis=dims[1][0])
    return lax.dot_general(a, b, (dims, ((), ())), preferred_element_type=jnp.float32)


def invert_tile(a):
    lane = lax.broadcasted_iota(jnp.int32, (STRIP, TILE), 1)
    sub = lax.broadcasted_iota(jnp.int32, (STRIP, TILE), 0)
    lane_all = lax.broadcasted_iota(jnp.int32, (TILE, TILE), 1)
    done = []
    for g in range(TILE // STRIP):
        lo = g * STRIP
        strip = a[:STRIP]
        cols = [
            jnp.broadcast_to(strip[:, lo + k : lo + k + 1], (STRIP, TILE)) for k in range(STRIP)
        ]
        t = jnp.where((lane >= lo) & (lane < lo + STRIP), (lane - lo == sub).astype(jnp.float32), strip)
        out = jnp.zeros_like(t)
        for j in range(STRIP):
            pivot = jnp.broadcast_to(cols[j][j : j + 1], (STRIP, TILE))
            inv = 1.0 / pivot
            row = jnp.broadcast_to(t[j : j + 1], (STRIP, TILE))
            out = jnp.where(sub == j, row * lax.rsqrt(pivot), out)
            mult = jnp.where(sub == j, 1.0 - inv, cols[j] * inv)
            t = t - mult * row
            for k in range(j + 1, STRIP):
                cols[k] = cols[k] - mult * jnp.broadcast_to(cols[k][j : j + 1], (STRIP, TILE))
        done.append(jnp.where(lane < lo + STRIP, out, 0.0))
        if lo + STRIP < TILE:
            below = a[STRIP:]
            rows = TILE - lo - STRIP
            inside = (lane_all[:rows] >= lo) & (lane_all[:rows] < lo + STRIP)
            sent = strip.T[lo + STRIP :]
            a = jnp.where(inside, 0.0, below) - dot3(sent, t)
    return jnp.concatenate(done, axis=0)


def inverse_kernel(d_ref, o_ref, w_ref):
    size = d_ref.shape[0]
    count = size // TILE
    w_ref[...] = d_ref[...]
    lane = lax.broadcasted_iota(jnp.int32, (TILE, size), 1)
    eye = (
        lax.broadcasted_iota(jnp.int32, (TILE, TILE), 0)
        == lax.broadcasted_iota(jnp.int32, (TILE, TILE), 1)
    ).astype(jnp.float32)

    def step(k, carry):
        at = pl.multiple_of(k * TILE, TILE)
        here = pl.ds(at, TILE)
        small = invert_tile(w_ref[here, here])
        w_ref[here, here] = eye
        z = dot3(small, w_ref[here, :])
        o_ref[here, :] = jnp.where(lane < at + TILE, z, 0.0)
        w_ref[here, :] = z
        zh, zl = halves(z)
        right = jnp.concatenate([zh, zl, zh], axis=0)

        def trail(i, c):
            mine = pl.ds(pl.multiple_of(i * TILE, TILE), TILE)
            yh, yl = halves(w_ref[here, mine].T)
            left = jnp.concatenate([yh, yh, yl], axis=1)
            w_ref[mine, here] = jnp.zeros((TILE, TILE), jnp.float32)
            w_ref[mine, :] -= jnp.dot(left, right, preferred_element_type=jnp.float32)
            return c

        lax.fori_loop(k + 1, count, trail, 0)
        return carry

    lax.fori_loop(0, count, step, 0)


def invert(diagonal):
    size = diagonal.shape[0]
    return pl.pallas_call(
        inverse_kernel,
        out_shape=jax.ShapeDtypeStruct((size, size), jnp.float32),
        in_specs=[pl.BlockSpec(memory_space=pltpu.VMEM)],
        out_specs=pl.BlockSpec(memory_space=pltpu.VMEM),
        scratch_shapes=[pltpu.VMEM((size, size), jnp.float32)],
        compiler_params=pltpu.CompilerParams(vmem_limit_bytes=40 * 1024 * 1024),
        cost_estimate=pl.CostEstimate(flops=4 * size**3, bytes_accessed=8 * size * size, transcendentals=0),
    )(diagonal)


def spread(value, axis, source):
    kept = jnp.where(lax.axis_index(axis) == source, value, 0).astype(value.dtype)
    return lax.psum(kept, axis)


def body(gram_panel, left_factor, solved_prev, right_block):
    row_count = lax.axis_size("row")
    col_count = lax.axis_size("col")
    row_place = lax.axis_index("row")
    col_place = lax.axis_index("col")
    block_rows = right_block.shape[0]
    col_width = gram_panel.shape[1]
    per_column = row_count // col_count
    strip_width = left_factor.shape[1] // per_column
    chosen = lax.all_gather(left_factor[:block_rows], "row", axis=0, tiled=True)
    portion = chosen
    summed = lax.psum_scatter(
        jnp.einsum("pk,mk->pm", portion, left_factor, preferred_element_type=jnp.float32),
        "col",
        scatter_dimension=0,
        tiled=True,
    )
    update = gram_panel - summed.T
    diag_part = lax.all_gather(update[:block_rows], "row", axis=0, tiled=True)
    diagonal = lax.all_gather(diag_part, "col", axis=1, tiled=True)
    inverse = invert(diagonal)
    inverse_cols = lax.dynamic_slice_in_dim(inverse, col_place * col_width, col_width, 0)
    inverse_part = inverse_cols
    panel_factor = lax.dot_general(
        lax.all_gather(update, "col", axis=1, tiled=True),
        inverse_part,
        (((1,), (1,)), ((), ())),
        precision=lax.Precision.HIGHEST,
    )
    strip_piece = lax.dynamic_slice_in_dim(
        chosen, row_place % per_column * strip_width, strip_width, 1
    )
    strip_piece = spread(strip_piece, "col", row_place // per_column)
    portion = strip_piece
    reduced = right_block - lax.psum_scatter(
        jnp.dot(portion, solved_prev, preferred_element_type=jnp.float32),
        "row",
        scatter_dimension=0,
        tiled=True,
    )
    inverse_rows = lax.dynamic_slice_in_dim(inverse, row_place * block_rows, block_rows, 0)
    inverse_part = inverse_rows
    solved_panel = jnp.dot(
        inverse_part,
        lax.all_gather(reduced, "row", axis=0, tiled=True),
        precision=lax.Precision.HIGHEST,
    )
    return (panel_factor, solved_panel)


def solution(mesh):
    in_specs = (P("row", "col"), P("row", "col"), P("row", "col"), P("row", "col"))
    out_specs = (P("row", "col"), P("row", "col"))
    return jax.shard_map(body, mesh=mesh, in_specs=in_specs, out_specs=out_specs, check_vma=False)
```

```python
import functools

import jax
import jax.numpy as jnp
from jax import lax
from jax.experimental import pallas as pl
from jax.experimental.pallas import tpu as pltpu
from jax.sharding import PartitionSpec as P

STRIP = 8
TILE = 128


def halves(value):
    high = value.astype(jnp.bfloat16)
    low = (value - high.astype(jnp.float32)).astype(jnp.bfloat16)
    return high, low


def dot3(left, right, dims=((1,), (0,))):
    lh, ll = halves(left)
    rh, rl = halves(right)
    a = jnp.concatenate([lh, lh, ll], axis=dims[0][0])
    b = jnp.concatenate([rh, rl, rh], axis=dims[1][0])
    return lax.dot_general(a, b, (dims, ((), ())), preferred_element_type=jnp.float32)


def invert_tile(a):
    lane = lax.broadcasted_iota(jnp.int32, (STRIP, TILE), 1)
    sub = lax.broadcasted_iota(jnp.int32, (STRIP, TILE), 0)
    lane_all = lax.broadcasted_iota(jnp.int32, (TILE, TILE), 1)
    done = []
    for g in range(TILE // STRIP):
        lo = g * STRIP
        strip = a[:STRIP]
        cols = [
            jnp.broadcast_to(strip[:, lo + k : lo + k + 1], (STRIP, TILE)) for k in range(STRIP)
        ]
        t = jnp.where((lane >= lo) & (lane < lo + STRIP), (lane - lo == sub).astype(jnp.float32), strip)
        out = jnp.zeros_like(t)
        for j in range(STRIP):
            pivot = jnp.broadcast_to(cols[j][j : j + 1], (STRIP, TILE))
            inv = 1.0 / pivot
            row = jnp.broadcast_to(t[j : j + 1], (STRIP, TILE))
            out = jnp.where(sub == j, row * lax.rsqrt(pivot), out)
            mult = jnp.where(sub == j, 1.0 - inv, cols[j] * inv)
            t = t - mult * row
            for k in range(j + 1, STRIP):
                cols[k] = cols[k] - mult * jnp.broadcast_to(cols[k][j : j + 1], (STRIP, TILE))
        done.append(jnp.where(lane < lo + STRIP, out, 0.0))
        if lo + STRIP < TILE:
            below = a[STRIP:]
            rows = TILE - lo - STRIP
            inside = (lane_all[:rows] >= lo) & (lane_all[:rows] < lo + STRIP)
            sent = strip.T[lo + STRIP :]
            a = jnp.where(inside, 0.0, below) - dot3(sent, t)
    return jnp.concatenate(done, axis=0)


def inverse_kernel(d_ref, o_ref, w_ref):
    size = d_ref.shape[0]
    count = size // TILE
    w_ref[...] = d_ref[...]
    lane = lax.broadcasted_iota(jnp.int32, (TILE, size), 1)
    eye = (
        lax.broadcasted_iota(jnp.int32, (TILE, TILE), 0)
        == lax.broadcasted_iota(jnp.int32, (TILE, TILE), 1)
    ).astype(jnp.float32)

    def step(k, carry):
        at = pl.multiple_of(k * TILE, TILE)
        here = pl.ds(at, TILE)
        small = invert_tile(w_ref[here, here])
        w_ref[here, here] = eye
        z = dot3(small, w_ref[here, :])
        o_ref[here, :] = jnp.where(lane < at + TILE, z, 0.0)
        w_ref[here, :] = z
        zh, zl = halves(z)
        right = jnp.concatenate([zh, zl, zh], axis=0)

        def trail(i, c):
            mine = pl.ds(pl.multiple_of(i * TILE, TILE), TILE)
            yh, yl = halves(w_ref[here, mine].T)
            left = jnp.concatenate([yh, yh, yl], axis=1)
            w_ref[mine, here] = jnp.zeros((TILE, TILE), jnp.float32)
            w_ref[mine, :] -= jnp.dot(left, right, preferred_element_type=jnp.float32)
            return c

        lax.fori_loop(k + 1, count, trail, 0)
        return carry

    lax.fori_loop(0, count, step, 0)


def invert(diagonal):
    size = diagonal.shape[0]
    return pl.pallas_call(
        inverse_kernel,
        out_shape=jax.ShapeDtypeStruct((size, size), jnp.float32),
        in_specs=[pl.BlockSpec(memory_space=pltpu.VMEM)],
        out_specs=pl.BlockSpec(memory_space=pltpu.VMEM),
        scratch_shapes=[pltpu.VMEM((size, size), jnp.float32)],
        compiler_params=pltpu.CompilerParams(vmem_limit_bytes=40 * 1024 * 1024),
        cost_estimate=pl.CostEstimate(flops=4 * size**3, bytes_accessed=8 * size * size, transcendentals=0),
    )(diagonal)


MESH = pl.DeviceIdType.MESH


def update_kernel(
    rows_n, cols_n, left_ref, gram_ref, d_ref, low_ref, chosen, top_out, top_in, low_out, low_in,
    top_all, low_all, c_send, c_recv, cs_send, cs_recv, t_send, t_recv, l_send, l_recv,
    z_send, z_recv, y_send, y_recv, d_send, d_recv, ds_send, ds_recv,
):
    b, w = top_all.shape[1], top_all.shape[2]
    pair = rows_n // cols_n
    chips = rows_n // pair
    r = lax.axis_index("row")
    c = lax.axis_index("col")
    core = r % pair
    p = r // pair
    sibling = p * pair + (pair - 1 - core)

    def peer(s):
        return ((p + s) % chips) * pair + core

    def origin(s):
        return (p + chips - s) % chips

    barrier = pltpu.get_barrier_semaphore()
    for s in range(1, chips):
        pl.semaphore_signal(barrier, inc=1, device_id=(peer(s), c), device_id_type=MESH)
    for u in range(1, cols_n):
        pl.semaphore_signal(barrier, inc=1, device_id=(r, (c + u) % cols_n), device_id_type=MESH)
    pl.semaphore_signal(barrier, inc=1, device_id=(sibling, c), device_id_type=MESH)
    pl.semaphore_wait(barrier, chips + cols_n - 1)

    def rows_of(ref, q):
        return ref.at[pl.ds(pl.multiple_of(q * b, b), b)]

    def copy(src, dst, send, recv, to):
        return pltpu.make_async_remote_copy(
            src_ref=src, dst_ref=dst, send_sem=send, recv_sem=recv, device_id=to, device_id_type=MESH
        )

    class Gather:
        def __init__(self, ref, own, send, recv, side_send, side_recv):
            self.ref, self.own = ref, own
            self.sems = (send, recv, side_send, side_recv)

        def far(self, s):
            send, recv = self.sems[:2]
            return copy(self.own, rows_of(self.ref, r), send.at[s], recv.at[s], (peer(s), c))

        def far_in(self, s):
            send, recv = self.sems[:2]
            block = rows_of(self.ref, origin(s) * pair + core)
            return copy(block, block, send.at[s], recv.at[s], (peer(s), c))

        def near(self, s):
            send, recv = self.sems[2:]
            block = rows_of(self.ref, origin(s) * pair + core)
            src = self.own if s == 0 else block
            return copy(src, block, send.at[s], recv.at[s], (sibling, c))

        def near_in(self, s):
            send, recv = self.sems[2:]
            block = rows_of(self.ref, origin(s) * pair + (pair - 1 - core))
            return copy(block, block, send.at[s], recv.at[s], (sibling, c))

        def start(self):
            for s in range(1, chips):
                self.far(s).start()
            self.near(0).start()

        def relay(self, s):
            if s > 0:
                self.far_in(s).wait_recv()
                self.near(s).start()

        def finish(self):
            for s in range(chips):
                if s > 0:
                    self.far(s).wait_send()
                self.near(s).wait_send()

    def to_owner(q, out, into, send, recv):
        return copy(out.at[q], into.at[c], send.at[q], recv.at[c], (r, q))

    def from_owner(q, out, into, send, recv):
        return copy(out.at[q], into.at[q], send.at[q], recv.at[q], (r, q))

    def product(rows, q):
        block = chosen[pl.ds(pl.multiple_of(q * w, w), w), :]
        return lax.dot_general(
            rows, block, (((1,), (1,)), ((), ())), preferred_element_type=jnp.float32
        )

    def total(start, out, into, sems):
        value = start - out[c]
        for u in range(1, cols_n):
            q = (c + u) % cols_n
            from_owner(q, out, into, *sems).wait_recv()
            value = value - into[q]
        return value

    def share(ref, send, recv, u):
        return copy(ref.at[c], ref.at[c], send.at[u], recv.at[u], (r, (c + u) % cols_n))

    def shared(ref, send, recv, u):
        block = ref.at[(c + cols_n - u) % cols_n]
        return copy(block, block, send.at[u], recv.at[u], (r, (c + u) % cols_n))

    top_sems, low_sems = (t_send, t_recv), (l_send, l_recv)
    gather = Gather(chosen, left_ref.at[pl.ds(0, b)], c_send, c_recv, cs_send, cs_recv)
    gather.start()
    rows_of(chosen, r)[...] = left_ref[:b]
    for s in range(chips):
        gather.relay(s)
        if s == 0:
            gather.near_in(0).wait_recv()
        for v in ((s,) if s < 1 else (s - 1,) if s > 1 else ()):
            if v > 0:
                gather.near_in(v).wait_recv()
            top_out[origin(v)] = product(left_ref[:b], origin(v))

            @pl.when(origin(v) != c)
            def _(v=v):
                to_owner(origin(v), top_out, top_in, *top_sems).start()

    if chips > 1:
        v = chips - 1
        gather.near_in(v).wait_recv()
        top_out[origin(v)] = product(left_ref[:b], origin(v))

        @pl.when(origin(v) != c)
        def _():
            to_owner(origin(v), top_out, top_in, *top_sems).start()

    for s in range(chips):
        low_out[origin(s)] = product(left_ref[b:], origin(s))
    top_all[c] = total(gram_ref[:b], top_out, top_in, top_sems)
    for u in range(1, cols_n):
        share(top_all, z_send, z_recv, u).start()
    for u in range(1, cols_n):
        q = (c + u) % cols_n
        to_owner(q, low_out, low_in, *low_sems).start()
    for u in range(1, cols_n):
        shared(top_all, z_send, z_recv, u).wait_recv()
    for q in range(cols_n):
        d_ref[pl.ds(pl.multiple_of(r * b, b), b), q * w : (q + 1) * w] = top_all[q]
    strips = Gather(d_ref, rows_of(d_ref, r), d_send, d_recv, ds_send, ds_recv)
    strips.start()
    low_all[c] = total(gram_ref[b:], low_out, low_in, low_sems)
    for u in range(1, cols_n):
        share(low_all, y_send, y_recv, u).start()
    for s in range(chips):
        strips.relay(s)
    for u in range(1, cols_n):
        shared(low_all, y_send, y_recv, u).wait_recv()
    for q in range(cols_n):
        low_ref[:, q * w : (q + 1) * w] = low_all[q]
    for s in range(chips):
        strips.near_in(s).wait_recv()
    strips.finish()
    gather.finish()
    for u in range(1, cols_n):
        q = (c + u) % cols_n
        to_owner(q, top_out, top_in, *top_sems).wait_send()
        to_owner(q, low_out, low_in, *low_sems).wait_send()
        share(top_all, z_send, z_recv, u).wait_send()
        share(low_all, y_send, y_recv, u).wait_send()


def updated(left_factor, gram_panel, b):
    rows_n, cols_n = lax.axis_size("row"), lax.axis_size("col")
    rows, w = gram_panel.shape
    size = rows_n * b
    f32 = jnp.float32
    vmem = pl.BlockSpec(memory_space=pltpu.VMEM)
    chips = pltpu.SemaphoreType.DMA((cols_n,))
    return pl.pallas_call(
        functools.partial(update_kernel, rows_n, cols_n),
        out_shape=(
            jax.ShapeDtypeStruct((size, size), f32),
            jax.ShapeDtypeStruct((rows - b, size), f32),
        ),
        in_specs=[vmem, vmem],
        out_specs=(vmem, vmem),
        scratch_shapes=[pltpu.VMEM((size, left_factor.shape[1]), jnp.bfloat16)]
        + [pltpu.VMEM((cols_n, b, w), f32)] * 2
        + [pltpu.VMEM((cols_n, rows - b, w), f32)] * 2
        + [pltpu.VMEM((cols_n, b, w), f32), pltpu.VMEM((cols_n, rows - b, w), f32)]
        + [chips] * 16,
        compiler_params=pltpu.CompilerParams(
            collective_id=0, has_side_effects=True, vmem_limit_bytes=48 * 1024 * 1024
        ),
        cost_estimate=pl.CostEstimate(flops=2 * size * rows * 1024, bytes_accessed=8 * 1024 * 1024, transcendentals=0),
    )(left_factor, gram_panel)


def body(gram_panel, left_factor, solved_prev, right_block):
    row_place = lax.axis_index("row")
    col_place = lax.axis_index("col")
    b = right_block.shape[0]
    w = gram_panel.shape[1]
    solved = lax.all_gather(solved_prev, "row", axis=0, tiled=True)
    mine = lax.all_gather(left_factor[:b], "col", axis=1, tiled=True)
    diagonal, low = updated(left_factor, gram_panel, b)
    reduced = right_block - jnp.dot(mine, solved, preferred_element_type=jnp.float32)
    reduced = lax.all_gather(reduced, "row", axis=0, tiled=True)
    inverse = invert(diagonal)
    top = lax.dynamic_slice_in_dim(diagonal, row_place * b, b, 0)
    panel_factor = lax.dot_general(
        jnp.concatenate([top, low], axis=0),
        lax.dynamic_slice_in_dim(inverse, col_place * w, w, 0),
        (((1,), (1,)), ((), ())),
        precision=lax.Precision.HIGH,
    )
    solved_panel = jnp.dot(
        lax.dynamic_slice_in_dim(inverse, row_place * b, b, 0),
        reduced,
        precision=lax.Precision.HIGH,
    )
    return (panel_factor, solved_panel)


def solution(mesh):
    in_specs = (P("row", "col"), P("row", "col"), P("row", "col"), P("row", "col"))
    out_specs = (P("row", "col"), P("row", "col"))
    return jax.shard_map(body, mesh=mesh, in_specs=in_specs, out_specs=out_specs, check_vma=False)
```

```python
import functools

import jax
import jax.numpy as jnp
from jax import lax
from jax.experimental import pallas as pl
from jax.experimental.pallas import tpu as pltpu
from jax.sharding import PartitionSpec as P

STRIP = 8
TILE = 128


def halves(value):
    high = value.astype(jnp.bfloat16)
    low = (value - high.astype(jnp.float32)).astype(jnp.bfloat16)
    return high, low


def dot3(left, right, dims=((1,), (0,))):
    lh, ll = halves(left)
    rh, rl = halves(right)
    a = jnp.concatenate([lh, lh, ll], axis=dims[0][0])
    b = jnp.concatenate([rh, rl, rh], axis=dims[1][0])
    return lax.dot_general(a, b, (dims, ((), ())), preferred_element_type=jnp.float32)


def invert_tile(a):
    lane = lax.broadcasted_iota(jnp.int32, (STRIP, TILE), 1)
    sub = lax.broadcasted_iota(jnp.int32, (STRIP, TILE), 0)
    lane_all = lax.broadcasted_iota(jnp.int32, (TILE, TILE), 1)
    done = []
    for g in range(TILE // STRIP):
        lo = g * STRIP
        strip = a[:STRIP]
        cols = [
            jnp.broadcast_to(strip[:, lo + k : lo + k + 1], (STRIP, TILE)) for k in range(STRIP)
        ]
        t = jnp.where((lane >= lo) & (lane < lo + STRIP), (lane - lo == sub).astype(jnp.float32), strip)
        out = jnp.zeros_like(t)
        for j in range(STRIP):
            pivot = jnp.broadcast_to(cols[j][j : j + 1], (STRIP, TILE))
            inv = 1.0 / pivot
            row = jnp.broadcast_to(t[j : j + 1], (STRIP, TILE))
            out = jnp.where(sub == j, row * lax.rsqrt(pivot), out)
            mult = jnp.where(sub == j, 1.0 - inv, cols[j] * inv)
            t = t - mult * row
            for k in range(j + 1, STRIP):
                cols[k] = cols[k] - mult * jnp.broadcast_to(cols[k][j : j + 1], (STRIP, TILE))
        done.append(jnp.where(lane < lo + STRIP, out, 0.0))
        if lo + STRIP < TILE:
            below = a[STRIP:]
            rows = TILE - lo - STRIP
            inside = (lane_all[:rows] >= lo) & (lane_all[:rows] < lo + STRIP)
            sent = strip.T[lo + STRIP :]
            a = jnp.where(inside, 0.0, below) - dot3(sent, t)
    return jnp.concatenate(done, axis=0)


def inverse_kernel(d_ref, o_ref, w_ref):
    size = d_ref.shape[0]
    count = size // TILE
    w_ref[...] = d_ref[...]
    lane = lax.broadcasted_iota(jnp.int32, (TILE, size), 1)
    eye = (
        lax.broadcasted_iota(jnp.int32, (TILE, TILE), 0)
        == lax.broadcasted_iota(jnp.int32, (TILE, TILE), 1)
    ).astype(jnp.float32)

    def step(k, carry):
        at = pl.multiple_of(k * TILE, TILE)
        here = pl.ds(at, TILE)
        small = invert_tile(w_ref[here, here])
        w_ref[here, here] = eye
        z = dot3(small, w_ref[here, :])
        o_ref[here, :] = jnp.where(lane < at + TILE, z, 0.0)
        w_ref[here, :] = z
        zh, zl = halves(z)
        right = jnp.concatenate([zh, zl, zh], axis=0)

        def trail(i, c):
            mine = pl.ds(pl.multiple_of(i * TILE, TILE), TILE)
            yh, yl = halves(w_ref[here, mine].T)
            left = jnp.concatenate([yh, yh, yl], axis=1)
            w_ref[mine, here] = jnp.zeros((TILE, TILE), jnp.float32)
            w_ref[mine, :] -= jnp.dot(left, right, preferred_element_type=jnp.float32)
            return c

        lax.fori_loop(k + 1, count, trail, 0)
        return carry

    lax.fori_loop(0, count, step, 0)


def invert(diagonal):
    size = diagonal.shape[0]
    return pl.pallas_call(
        inverse_kernel,
        out_shape=jax.ShapeDtypeStruct((size, size), jnp.float32),
        in_specs=[pl.BlockSpec(memory_space=pltpu.VMEM)],
        out_specs=pl.BlockSpec(memory_space=pltpu.VMEM),
        scratch_shapes=[pltpu.VMEM((size, size), jnp.float32)],
        compiler_params=pltpu.CompilerParams(vmem_limit_bytes=40 * 1024 * 1024),
        cost_estimate=pl.CostEstimate(flops=4 * size**3, bytes_accessed=192 * size * size, transcendentals=0),
    )(diagonal)


MESH = pl.DeviceIdType.MESH


def update_kernel(
    rows_n, cols_n, left_ref, gram_ref, d_ref, low_ref, chosen, top_out, top_in, low_out, low_in,
    top_all, low_all, c_send, c_recv, cs_send, cs_recv, t_send, t_recv, l_send, l_recv,
    z_send, z_recv, y_send, y_recv, d_send, d_recv, ds_send, ds_recv,
):
    b, w = top_all.shape[1], top_all.shape[2]
    pair = rows_n // cols_n
    chips = rows_n // pair
    r = lax.axis_index("row")
    c = lax.axis_index("col")
    core = r % pair
    p = r // pair
    sibling = p * pair + (pair - 1 - core)

    def peer(s):
        return ((p + s) % chips) * pair + core

    def origin(s):
        return (p + chips - s) % chips

    barrier = pltpu.get_barrier_semaphore()
    for s in range(1, chips):
        pl.semaphore_signal(barrier, inc=1, device_id=(peer(s), c), device_id_type=MESH)
    for u in range(1, cols_n):
        pl.semaphore_signal(barrier, inc=1, device_id=(r, (c + u) % cols_n), device_id_type=MESH)
    pl.semaphore_signal(barrier, inc=1, device_id=(sibling, c), device_id_type=MESH)
    pl.semaphore_wait(barrier, chips + cols_n - 1)

    def rows_of(ref, q):
        return ref.at[pl.ds(pl.multiple_of(q * b, b), b)]

    def copy(src, dst, send, recv, to):
        return pltpu.make_async_remote_copy(
            src_ref=src, dst_ref=dst, send_sem=send, recv_sem=recv, device_id=to, device_id_type=MESH
        )

    class Gather:
        def __init__(self, ref, own, send, recv, side_send, side_recv):
            self.ref, self.own = ref, own
            self.sems = (send, recv, side_send, side_recv)

        def far(self, s):
            send, recv = self.sems[:2]
            return copy(self.own, rows_of(self.ref, r), send.at[s], recv.at[s], (peer(s), c))

        def far_in(self, s):
            send, recv = self.sems[:2]
            block = rows_of(self.ref, origin(s) * pair + core)
            return copy(block, block, send.at[s], recv.at[s], (peer(s), c))

        def near(self, s):
            send, recv = self.sems[2:]
            block = rows_of(self.ref, origin(s) * pair + core)
            src = self.own if s == 0 else block
            return copy(src, block, send.at[s], recv.at[s], (sibling, c))

        def near_in(self, s):
            send, recv = self.sems[2:]
            block = rows_of(self.ref, origin(s) * pair + (pair - 1 - core))
            return copy(block, block, send.at[s], recv.at[s], (sibling, c))

        def start(self):
            for s in range(1, chips):
                self.far(s).start()
            self.near(0).start()

        def relay(self, s):
            if s > 0:
                self.far_in(s).wait_recv()
                self.near(s).start()

        def finish(self):
            for s in range(chips):
                if s > 0:
                    self.far(s).wait_send()
                self.near(s).wait_send()

    def to_owner(q, out, into, send, recv):
        return copy(out.at[q], into.at[c], send.at[q], recv.at[c], (r, q))

    def from_owner(q, out, into, send, recv):
        return copy(out.at[q], into.at[q], send.at[q], recv.at[q], (r, q))

    def product(rows, q):
        block = chosen[pl.ds(pl.multiple_of(q * w, w), w), :]
        return lax.dot_general(
            rows, block, (((1,), (1,)), ((), ())), preferred_element_type=jnp.float32
        )

    def total(start, out, into, sems):
        value = start - out[c]
        for u in range(1, cols_n):
            q = (c + u) % cols_n
            from_owner(q, out, into, *sems).wait_recv()
            value = value - into[q]
        return value

    def share(ref, send, recv, u):
        return copy(ref.at[c], ref.at[c], send.at[u], recv.at[u], (r, (c + u) % cols_n))

    def shared(ref, send, recv, u):
        block = ref.at[(c + cols_n - u) % cols_n]
        return copy(block, block, send.at[u], recv.at[u], (r, (c + u) % cols_n))

    top_sems, low_sems = (t_send, t_recv), (l_send, l_recv)
    gather = Gather(chosen, left_ref.at[pl.ds(0, b)], c_send, c_recv, cs_send, cs_recv)
    gather.start()
    rows_of(chosen, r)[...] = left_ref[:b]
    for s in range(chips):
        gather.relay(s)
        if s == 0:
            gather.near_in(0).wait_recv()
        for v in ((s,) if s < 1 else (s - 1,) if s > 1 else ()):
            if v > 0:
                gather.near_in(v).wait_recv()
            top_out[origin(v)] = product(left_ref[:b], origin(v))

            @pl.when(origin(v) != c)
            def _(v=v):
                to_owner(origin(v), top_out, top_in, *top_sems).start()

    if chips > 1:
        v = chips - 1
        gather.near_in(v).wait_recv()
        top_out[origin(v)] = product(left_ref[:b], origin(v))

        @pl.when(origin(v) != c)
        def _():
            to_owner(origin(v), top_out, top_in, *top_sems).start()

    for s in range(chips):
        low_out[origin(s)] = product(left_ref[b:], origin(s))
    top_all[c] = total(gram_ref[:b], top_out, top_in, top_sems)
    for u in range(1, cols_n):
        share(top_all, z_send, z_recv, u).start()
    for u in range(1, cols_n):
        q = (c + u) % cols_n
        to_owner(q, low_out, low_in, *low_sems).start()
    for u in range(1, cols_n):
        shared(top_all, z_send, z_recv, u).wait_recv()
    for q in range(cols_n):
        d_ref[pl.ds(pl.multiple_of(r * b, b), b), q * w : (q + 1) * w] = top_all[q]
    strips = Gather(d_ref, rows_of(d_ref, r), d_send, d_recv, ds_send, ds_recv)
    strips.start()
    low_all[c] = total(gram_ref[b:], low_out, low_in, low_sems)
    for u in range(1, cols_n):
        share(low_all, y_send, y_recv, u).start()
    for s in range(chips):
        strips.relay(s)
    for u in range(1, cols_n):
        shared(low_all, y_send, y_recv, u).wait_recv()
    for q in range(cols_n):
        low_ref[:, q * w : (q + 1) * w] = low_all[q]
    for s in range(chips):
        strips.near_in(s).wait_recv()
    strips.finish()
    gather.finish()
    for u in range(1, cols_n):
        q = (c + u) % cols_n
        to_owner(q, top_out, top_in, *top_sems).wait_send()
        to_owner(q, low_out, low_in, *low_sems).wait_send()
        share(top_all, z_send, z_recv, u).wait_send()
        share(low_all, y_send, y_recv, u).wait_send()


def updated(left_factor, gram_panel, b):
    rows_n, cols_n = lax.axis_size("row"), lax.axis_size("col")
    rows, w = gram_panel.shape
    size = rows_n * b
    f32 = jnp.float32
    vmem = pl.BlockSpec(memory_space=pltpu.VMEM)
    chips = pltpu.SemaphoreType.DMA((cols_n,))
    return pl.pallas_call(
        functools.partial(update_kernel, rows_n, cols_n),
        out_shape=(
            jax.ShapeDtypeStruct((size, size), f32),
            jax.ShapeDtypeStruct((rows - b, size), f32),
        ),
        in_specs=[vmem, vmem],
        out_specs=(vmem, vmem),
        scratch_shapes=[pltpu.VMEM((size, left_factor.shape[1]), jnp.bfloat16)]
        + [pltpu.VMEM((cols_n, b, w), f32)] * 2
        + [pltpu.VMEM((cols_n, rows - b, w), f32)] * 2
        + [pltpu.VMEM((cols_n, b, w), f32), pltpu.VMEM((cols_n, rows - b, w), f32)]
        + [chips] * 16,
        compiler_params=pltpu.CompilerParams(
            collective_id=0, has_side_effects=True, vmem_limit_bytes=48 * 1024 * 1024
        ),
        cost_estimate=pl.CostEstimate(flops=2 * size * rows * 1024, bytes_accessed=256 * size * size, transcendentals=0),
    )(left_factor, gram_panel)


def body(gram_panel, left_factor, solved_prev, right_block):
    row_place = lax.axis_index("row")
    col_place = lax.axis_index("col")
    b = right_block.shape[0]
    w = gram_panel.shape[1]
    solved = lax.all_gather(solved_prev, "row", axis=0, tiled=True)
    mine = lax.all_gather(left_factor[:b], "col", axis=1, tiled=True)
    diagonal, low = updated(left_factor, gram_panel, b)
    solved, mine, diagonal, low = lax.optimization_barrier((solved, mine, diagonal, low))
    reduced = right_block - jnp.dot(mine, solved, preferred_element_type=jnp.float32)
    reduced = lax.all_gather(reduced, "row", axis=0, tiled=True)
    inverse = invert(diagonal)
    top = lax.dynamic_slice_in_dim(diagonal, row_place * b, b, 0)
    panel_factor = lax.dot_general(
        jnp.concatenate([top, low], axis=0),
        lax.dynamic_slice_in_dim(inverse, col_place * w, w, 0),
        (((1,), (1,)), ((), ())),
        precision=lax.Precision.HIGH,
    )
    solved_panel = jnp.dot(
        lax.dynamic_slice_in_dim(inverse, row_place * b, b, 0),
        reduced,
        precision=lax.Precision.HIGH,
    )
    return (panel_factor, solved_panel)


def solution(mesh):
    in_specs = (P("row", "col"), P("row", "col"), P("row", "col"), P("row", "col"))
    out_specs = (P("row", "col"), P("row", "col"))
    return jax.shard_map(body, mesh=mesh, in_specs=in_specs, out_specs=out_specs, check_vma=False)
```

```python
import functools

import jax
import jax.numpy as jnp
from jax import lax
from jax.experimental import pallas as pl
from jax.experimental.pallas import tpu as pltpu
from jax.sharding import PartitionSpec as P

STRIP = 8
TILE = 128


def halves(value):
    high = value.astype(jnp.bfloat16)
    low = (value - high.astype(jnp.float32)).astype(jnp.bfloat16)
    return high, low


def dot3(left, right, dims=((1,), (0,))):
    lh, ll = halves(left)
    rh, rl = halves(right)
    a = jnp.concatenate([lh, lh, ll], axis=dims[0][0])
    b = jnp.concatenate([rh, rl, rh], axis=dims[1][0])
    return lax.dot_general(a, b, (dims, ((), ())), preferred_element_type=jnp.float32)


def reciprocal(value):
    guess = pl.reciprocal(value, approx=True)
    return guess * (2.0 - value * guess)


def spread_row(value, j):
    return jnp.broadcast_to(value[j : j + 1], (STRIP, TILE))


def spread_lane(value, k):
    return jnp.broadcast_to(value[:, k : k + 1], (STRIP, TILE))


def invert_tile(a):
    lane = lax.broadcasted_iota(jnp.int32, (STRIP, TILE), 1)
    sub = lax.broadcasted_iota(jnp.int32, (STRIP, TILE), 0)
    lane_all = lax.broadcasted_iota(jnp.int32, (TILE, TILE), 1)
    done = []
    strip, below = a[:STRIP], a[STRIP:]
    for g in range(TILE // STRIP):
        lo = g * STRIP
        hi = lo + STRIP
        cols = [spread_lane(strip, lo + k) for k in range(STRIP)]
        t = jnp.where((lane >= lo) & (lane < hi), (lane - lo == sub).astype(jnp.float32), strip)
        out = jnp.zeros_like(t)
        for j in range(0, STRIP, 2):
            p11, p12, p22 = spread_row(cols[j], j), spread_row(cols[j + 1], j), spread_row(cols[j + 1], j + 1)
            det = p11 * p22 - p12 * p12
            inv = reciprocal(det)
            row1, row2 = spread_row(t, j), spread_row(t, j + 1)
            root = lax.rsqrt(p11)
            out = jnp.where(sub == j, row1 * root, out)
            out = jnp.where(sub == j + 1, (row2 * p11 - row1 * p12) * (root * lax.rsqrt(det)), out)
            one = (cols[j] * p22 - cols[j + 1] * p12) * inv
            two = (cols[j + 1] * p11 - cols[j] * p12) * inv
            cross = p12 * inv
            one = jnp.where(sub == j, 1.0 - p22 * inv, jnp.where(sub == j + 1, cross, one))
            two = jnp.where(sub == j, cross, jnp.where(sub == j + 1, 1.0 - p11 * inv, two))
            t = t - one * row1 - two * row2
            for k in range(j + 2, STRIP):
                cols[k] = cols[k] - one * spread_row(cols[k], j) - two * spread_row(cols[k], j + 1)
        done.append(jnp.where(lane < hi, out, 0.0))
        if hi < TILE:
            sent = strip.T[hi:]
            strip = jnp.where((lane >= lo) & (lane < hi), 0.0, below[:STRIP])
            for k in range(STRIP):
                strip = strip - spread_lane(sent[:STRIP], k) * spread_row(t, k)
            if hi + STRIP < TILE:
                inside = lane_all[: TILE - hi - STRIP]
                inside = (inside >= lo) & (inside < hi)
                below = jnp.where(inside, 0.0, below[STRIP:]) - dot3(sent[STRIP:], t)
    return jnp.concatenate(done, axis=0)


def inverse_kernel(d_ref, o_ref, w_ref):
    size = d_ref.shape[0]
    count = size // TILE
    w_ref[...] = d_ref[...]
    lane = lax.broadcasted_iota(jnp.int32, (TILE, size), 1)
    eye = (
        lax.broadcasted_iota(jnp.int32, (TILE, TILE), 0)
        == lax.broadcasted_iota(jnp.int32, (TILE, TILE), 1)
    ).astype(jnp.float32)

    def step(k, carry):
        at = pl.multiple_of(k * TILE, TILE)
        here = pl.ds(at, TILE)
        small = invert_tile(w_ref[here, here])
        w_ref[here, here] = eye
        z = dot3(small, w_ref[here, :])
        o_ref[here, :] = jnp.where(lane < at + TILE, z, 0.0)
        w_ref[here, :] = z
        zh, zl = halves(z)
        right = jnp.concatenate([zh, zl, zh], axis=0)

        def trail(i, c):
            mine = pl.ds(pl.multiple_of(i * TILE, TILE), TILE)
            yh, yl = halves(w_ref[here, mine].T)
            left = jnp.concatenate([yh, yh, yl], axis=1)
            w_ref[mine, here] = jnp.zeros((TILE, TILE), jnp.float32)
            w_ref[mine, :] -= jnp.dot(left, right, preferred_element_type=jnp.float32)
            return c

        lax.fori_loop(k + 1, count, trail, 0)
        return carry

    lax.fori_loop(0, count, step, 0)


def invert(diagonal):
    size = diagonal.shape[0]
    return pl.pallas_call(
        inverse_kernel,
        out_shape=jax.ShapeDtypeStruct((size, size), jnp.float32),
        in_specs=[pl.BlockSpec(memory_space=pltpu.VMEM)],
        out_specs=pl.BlockSpec(memory_space=pltpu.VMEM),
        scratch_shapes=[pltpu.VMEM((size, size), jnp.float32)],
        compiler_params=pltpu.CompilerParams(vmem_limit_bytes=40 * 1024 * 1024),
        cost_estimate=pl.CostEstimate(flops=4 * size**3, bytes_accessed=192 * size * size, transcendentals=0),
    )(diagonal)


MESH = pl.DeviceIdType.MESH


def update_kernel(
    rows_n, cols_n, left_ref, gram_ref, d_ref, low_ref, chosen, top_out, top_in, low_out, low_in,
    top_all, low_all, c_send, c_recv, cs_send, cs_recv, t_send, t_recv, l_send, l_recv,
    z_send, z_recv, y_send, y_recv, d_send, d_recv, ds_send, ds_recv,
):
    b, w = top_all.shape[1], top_all.shape[2]
    pair = rows_n // cols_n
    chips = rows_n // pair
    r = lax.axis_index("row")
    c = lax.axis_index("col")
    core = r % pair
    p = r // pair
    sibling = p * pair + (pair - 1 - core)

    def peer(s):
        return ((p + s) % chips) * pair + core

    def origin(s):
        return (p + chips - s) % chips

    barrier = pltpu.get_barrier_semaphore()
    for s in range(1, chips):
        pl.semaphore_signal(barrier, inc=1, device_id=(peer(s), c), device_id_type=MESH)
    for u in range(1, cols_n):
        pl.semaphore_signal(barrier, inc=1, device_id=(r, (c + u) % cols_n), device_id_type=MESH)
    pl.semaphore_signal(barrier, inc=1, device_id=(sibling, c), device_id_type=MESH)
    pl.semaphore_wait(barrier, chips + cols_n - 1)

    def rows_of(ref, q):
        return ref.at[pl.ds(pl.multiple_of(q * b, b), b)]

    def copy(src, dst, send, recv, to):
        return pltpu.make_async_remote_copy(
            src_ref=src, dst_ref=dst, send_sem=send, recv_sem=recv, device_id=to, device_id_type=MESH
        )

    class Gather:
        def __init__(self, ref, own, send, recv, side_send, side_recv):
            self.ref, self.own = ref, own
            self.sems = (send, recv, side_send, side_recv)

        def far(self, s):
            send, recv = self.sems[:2]
            return copy(self.own, rows_of(self.ref, r), send.at[s], recv.at[s], (peer(s), c))

        def far_in(self, s):
            send, recv = self.sems[:2]
            block = rows_of(self.ref, origin(s) * pair + core)
            return copy(block, block, send.at[s], recv.at[s], (peer(s), c))

        def near(self, s):
            send, recv = self.sems[2:]
            block = rows_of(self.ref, origin(s) * pair + core)
            src = self.own if s == 0 else block
            return copy(src, block, send.at[s], recv.at[s], (sibling, c))

        def near_in(self, s):
            send, recv = self.sems[2:]
            block = rows_of(self.ref, origin(s) * pair + (pair - 1 - core))
            return copy(block, block, send.at[s], recv.at[s], (sibling, c))

        def start(self):
            for s in range(1, chips):
                self.far(s).start()
            self.near(0).start()

        def relay(self, s):
            if s > 0:
                self.far_in(s).wait_recv()
                self.near(s).start()

        def finish(self):
            for s in range(chips):
                if s > 0:
                    self.far(s).wait_send()
                self.near(s).wait_send()

    def to_owner(q, out, into, send, recv):
        return copy(out.at[q], into.at[c], send.at[q], recv.at[c], (r, q))

    def from_owner(q, out, into, send, recv):
        return copy(out.at[q], into.at[q], send.at[q], recv.at[q], (r, q))

    def product(rows, q):
        block = chosen[pl.ds(pl.multiple_of(q * w, w), w), :]
        return lax.dot_general(
            rows, block, (((1,), (1,)), ((), ())), preferred_element_type=jnp.float32
        )

    def total(start, out, into, sems):
        value = start - out[c]
        for u in range(1, cols_n):
            q = (c + u) % cols_n
            from_owner(q, out, into, *sems).wait_recv()
            value = value - into[q]
        return value

    def share(ref, send, recv, u):
        return copy(ref.at[c], ref.at[c], send.at[u], recv.at[u], (r, (c + u) % cols_n))

    def shared(ref, send, recv, u):
        block = ref.at[(c + cols_n - u) % cols_n]
        return copy(block, block, send.at[u], recv.at[u], (r, (c + u) % cols_n))

    top_sems, low_sems = (t_send, t_recv), (l_send, l_recv)
    gather = Gather(chosen, left_ref.at[pl.ds(0, b)], c_send, c_recv, cs_send, cs_recv)
    gather.start()
    rows_of(chosen, r)[...] = left_ref[:b]
    for s in range(chips):
        gather.relay(s)
        if s == 0:
            gather.near_in(0).wait_recv()
        for v in ((s,) if s < 1 else (s - 1,) if s > 1 else ()):
            if v > 0:
                gather.near_in(v).wait_recv()
            top_out[origin(v)] = product(left_ref[:b], origin(v))

            @pl.when(origin(v) != c)
            def _(v=v):
                to_owner(origin(v), top_out, top_in, *top_sems).start()

    if chips > 1:
        v = chips - 1
        gather.near_in(v).wait_recv()
        top_out[origin(v)] = product(left_ref[:b], origin(v))

        @pl.when(origin(v) != c)
        def _():
            to_owner(origin(v), top_out, top_in, *top_sems).start()

    for s in range(chips):
        low_out[origin(s)] = product(left_ref[b:], origin(s))
    top_all[c] = total(gram_ref[:b], top_out, top_in, top_sems)
    for u in range(1, cols_n):
        share(top_all, z_send, z_recv, u).start()
    for u in range(1, cols_n):
        q = (c + u) % cols_n
        to_owner(q, low_out, low_in, *low_sems).start()
    for u in range(1, cols_n):
        shared(top_all, z_send, z_recv, u).wait_recv()
    for q in range(cols_n):
        d_ref[pl.ds(pl.multiple_of(r * b, b), b), q * w : (q + 1) * w] = top_all[q]
    strips = Gather(d_ref, rows_of(d_ref, r), d_send, d_recv, ds_send, ds_recv)
    strips.start()
    low_all[c] = total(gram_ref[b:], low_out, low_in, low_sems)
    for u in range(1, cols_n):
        share(low_all, y_send, y_recv, u).start()
    for s in range(chips):
        strips.relay(s)
    for u in range(1, cols_n):
        shared(low_all, y_send, y_recv, u).wait_recv()
    for q in range(cols_n):
        low_ref[:, q * w : (q + 1) * w] = low_all[q]
    for s in range(chips):
        strips.near_in(s).wait_recv()
    strips.finish()
    gather.finish()
    for u in range(1, cols_n):
        q = (c + u) % cols_n
        to_owner(q, top_out, top_in, *top_sems).wait_send()
        to_owner(q, low_out, low_in, *low_sems).wait_send()
        share(top_all, z_send, z_recv, u).wait_send()
        share(low_all, y_send, y_recv, u).wait_send()


def updated(left_factor, gram_panel, b):
    rows_n, cols_n = lax.axis_size("row"), lax.axis_size("col")
    rows, w = gram_panel.shape
    size = rows_n * b
    f32 = jnp.float32
    vmem = pl.BlockSpec(memory_space=pltpu.VMEM)
    chips = pltpu.SemaphoreType.DMA((cols_n,))
    return pl.pallas_call(
        functools.partial(update_kernel, rows_n, cols_n),
        out_shape=(
            jax.ShapeDtypeStruct((size, size), f32),
            jax.ShapeDtypeStruct((rows - b, size), f32),
        ),
        in_specs=[vmem, vmem],
        out_specs=(vmem, vmem),
        scratch_shapes=[pltpu.VMEM((size, left_factor.shape[1]), jnp.bfloat16)]
        + [pltpu.VMEM((cols_n, b, w), f32)] * 2
        + [pltpu.VMEM((cols_n, rows - b, w), f32)] * 2
        + [pltpu.VMEM((cols_n, b, w), f32), pltpu.VMEM((cols_n, rows - b, w), f32)]
        + [chips] * 16,
        compiler_params=pltpu.CompilerParams(
            collective_id=0, has_side_effects=True, vmem_limit_bytes=48 * 1024 * 1024
        ),
        cost_estimate=pl.CostEstimate(flops=2 * size * rows * 1024, bytes_accessed=256 * size * size, transcendentals=0),
    )(left_factor, gram_panel)


def body(gram_panel, left_factor, solved_prev, right_block):
    row_place = lax.axis_index("row")
    col_place = lax.axis_index("col")
    b = right_block.shape[0]
    w = gram_panel.shape[1]
    solved = lax.all_gather(solved_prev, "row", axis=0, tiled=True)
    mine = lax.all_gather(left_factor[:b], "col", axis=1, tiled=True)
    diagonal, low = updated(left_factor, gram_panel, b)
    solved, mine, diagonal, low = lax.optimization_barrier((solved, mine, diagonal, low))
    reduced = right_block - jnp.dot(mine, solved, preferred_element_type=jnp.float32)
    reduced = lax.all_gather(reduced, "row", axis=0, tiled=True)
    inverse = invert(diagonal)
    top = lax.dynamic_slice_in_dim(diagonal, row_place * b, b, 0)
    panel_factor = lax.dot_general(
        jnp.concatenate([top, low], axis=0),
        lax.dynamic_slice_in_dim(inverse, col_place * w, w, 0),
        (((1,), (1,)), ((), ())),
        precision=lax.Precision.HIGH,
    )
    solved_panel = jnp.dot(
        lax.dynamic_slice_in_dim(inverse, row_place * b, b, 0),
        reduced,
        precision=lax.Precision.HIGH,
    )
    return (panel_factor, solved_panel)


def solution(mesh):
    in_specs = (P("row", "col"), P("row", "col"), P("row", "col"), P("row", "col"))
    out_specs = (P("row", "col"), P("row", "col"))
    return jax.shard_map(body, mesh=mesh, in_specs=in_specs, out_specs=out_specs, check_vma=False)
```

```python
import functools

import jax
import jax.numpy as jnp
from jax import lax
from jax.experimental import pallas as pl
from jax.experimental.pallas import tpu as pltpu
from jax.sharding import PartitionSpec as P

STRIP = 8
TILE = 128


def halves(value):
    high = value.astype(jnp.bfloat16)
    low = (value - high.astype(jnp.float32)).astype(jnp.bfloat16)
    return high, low


def dot3(left, right, dims=((1,), (0,))):
    lh, ll = halves(left)
    rh, rl = halves(right)
    a = jnp.concatenate([lh, lh, ll], axis=dims[0][0])
    b = jnp.concatenate([rh, rl, rh], axis=dims[1][0])
    return lax.dot_general(a, b, (dims, ((), ())), preferred_element_type=jnp.float32)


def reciprocal(value):
    guess = pl.reciprocal(value, approx=True)
    return guess * (2.0 - value * guess)


def spread_row(value, j):
    return jnp.broadcast_to(value[j : j + 1], (STRIP, TILE))


def spread_lane(value, k):
    return jnp.broadcast_to(value[:, k : k + 1], (STRIP, TILE))


def invert_tile(a):
    lane = lax.broadcasted_iota(jnp.int32, (STRIP, TILE), 1)
    sub = lax.broadcasted_iota(jnp.int32, (STRIP, TILE), 0)
    lane_all = lax.broadcasted_iota(jnp.int32, (TILE, TILE), 1)
    done = []
    strip, below = a[:STRIP], a[STRIP:]
    for g in range(TILE // STRIP):
        lo = g * STRIP
        hi = lo + STRIP
        cols = [spread_lane(strip, lo + k) for k in range(STRIP)]
        t = jnp.where((lane >= lo) & (lane < hi), (lane - lo == sub).astype(jnp.float32), strip)
        out = jnp.zeros_like(t)
        for j in range(0, STRIP, 2):
            p11, p12, p22 = spread_row(cols[j], j), spread_row(cols[j + 1], j), spread_row(cols[j + 1], j + 1)
            det = p11 * p22 - p12 * p12
            inv = reciprocal(det)
            row1, row2 = spread_row(t, j), spread_row(t, j + 1)
            root = lax.rsqrt(p11)
            out = jnp.where(sub == j, row1 * root, out)
            out = jnp.where(sub == j + 1, (row2 * p11 - row1 * p12) * (root * lax.rsqrt(det)), out)
            one = (cols[j] * p22 - cols[j + 1] * p12) * inv
            two = (cols[j + 1] * p11 - cols[j] * p12) * inv
            cross = p12 * inv
            one = jnp.where(sub == j, 1.0 - p22 * inv, jnp.where(sub == j + 1, cross, one))
            two = jnp.where(sub == j, cross, jnp.where(sub == j + 1, 1.0 - p11 * inv, two))
            t = t - one * row1 - two * row2
            for k in range(j + 2, STRIP):
                cols[k] = cols[k] - one * spread_row(cols[k], j) - two * spread_row(cols[k], j + 1)
        done.append(jnp.where(lane < hi, out, 0.0))
        if hi < TILE:
            sent = strip.T[hi:]
            strip = jnp.where((lane >= lo) & (lane < hi), 0.0, below[:STRIP])
            for k in range(STRIP):
                strip = strip - spread_lane(sent[:STRIP], k) * spread_row(t, k)
            if hi + STRIP < TILE:
                inside = lane_all[: TILE - hi - STRIP]
                inside = (inside >= lo) & (inside < hi)
                below = jnp.where(inside, 0.0, below[STRIP:]) - dot3(sent[STRIP:], t)
    return jnp.concatenate(done, axis=0)


def inverse_kernel(d_ref, o_ref, w_ref):
    pieces, size, width = d_ref.shape
    count = size // TILE
    for q in range(pieces):
        w_ref[:, q * width : (q + 1) * width] = d_ref[q]
    lane = lax.broadcasted_iota(jnp.int32, (TILE, size), 1)
    eye = (
        lax.broadcasted_iota(jnp.int32, (TILE, TILE), 0)
        == lax.broadcasted_iota(jnp.int32, (TILE, TILE), 1)
    ).astype(jnp.float32)

    def step(k, carry):
        at = pl.multiple_of(k * TILE, TILE)
        here = pl.ds(at, TILE)
        small = invert_tile(w_ref[here, here])
        w_ref[here, here] = eye
        z = dot3(small, w_ref[here, :])
        o_ref[here, :] = jnp.where(lane < at + TILE, z, 0.0)
        w_ref[here, :] = z
        zh, zl = halves(z)
        right = jnp.concatenate([zh, zl, zh], axis=0)

        def trail(i, c):
            mine = pl.ds(pl.multiple_of(i * TILE, TILE), TILE)
            yh, yl = halves(w_ref[here, mine].T)
            left = jnp.concatenate([yh, yh, yl], axis=1)
            w_ref[mine, here] = jnp.zeros((TILE, TILE), jnp.float32)
            w_ref[mine, :] -= jnp.dot(left, right, preferred_element_type=jnp.float32)
            return c

        lax.fori_loop(k + 1, count, trail, 0)
        return carry

    lax.fori_loop(0, count, step, 0)


def invert(diagonal):
    size = diagonal.shape[1]
    return pl.pallas_call(
        inverse_kernel,
        out_shape=jax.ShapeDtypeStruct((size, size), jnp.float32),
        in_specs=[pl.BlockSpec(memory_space=pltpu.VMEM)],
        out_specs=pl.BlockSpec(memory_space=pltpu.VMEM),
        scratch_shapes=[pltpu.VMEM((size, size), jnp.float32)],
        compiler_params=pltpu.CompilerParams(vmem_limit_bytes=40 * 1024 * 1024),
        cost_estimate=pl.CostEstimate(flops=4 * size**3, bytes_accessed=192 * size * size, transcendentals=0),
    )(diagonal)


MESH = pl.DeviceIdType.MESH


def copy(src, dst, send, recv, to):
    return pltpu.make_async_remote_copy(
        src_ref=src, dst_ref=dst, send_sem=send, recv_sem=recv, device_id=to, device_id_type=MESH
    )


class Place:
    def __init__(self, rows_n, cols_n):
        self.cols_n = cols_n
        self.pair = rows_n // cols_n
        self.chips = rows_n // self.pair
        self.r = lax.axis_index("row")
        self.c = lax.axis_index("col")
        self.core = self.r % self.pair
        self.p = self.r // self.pair
        self.sibling = (self.p * self.pair + (self.pair - 1 - self.core), self.c)

    def peer(self, s):
        return (((self.p + s) % self.chips) * self.pair + self.core, self.c)

    def origin(self, s):
        return (self.p + self.chips - s) % self.chips


class RowGather:
    def __init__(self, at, own, block, send, recv, side_send, side_recv):
        self.at, self.own, self.block = at, own, block
        self.send, self.recv, self.side_send, self.side_recv = send, recv, side_send, side_recv

    def far(self, s):
        at = self.at
        return copy(self.own, self.block(at.r), self.send(s), self.recv(s), at.peer(s))

    def far_in(self, s):
        at = self.at
        block = self.block(at.origin(s) * at.pair + at.core)
        return copy(block, block, self.send(s), self.recv(s), at.peer(s))

    def near(self, s):
        at = self.at
        block = self.block(at.origin(s) * at.pair + at.core)
        src = self.own if s == 0 else block
        return copy(src, block, self.side_send(s), self.side_recv(s), at.sibling)

    def near_in(self, s):
        at = self.at
        block = self.block(at.origin(s) * at.pair + (at.pair - 1 - at.core))
        return copy(block, block, self.side_send(s), self.side_recv(s), at.sibling)

    def start(self):
        for s in range(1, self.at.chips):
            self.far(s).start()
        self.near(0).start()

    def relay(self, s):
        if s > 0:
            self.far_in(s).wait_recv()
            self.near(s).start()

    def relay_all(self):
        for s in range(1, self.at.chips):
            self.relay(s)

    def arrive(self):
        for s in range(self.at.chips):
            self.near_in(s).wait_recv()

    def finish(self):
        for s in range(self.at.chips):
            if s > 0:
                self.far(s).wait_send()
            self.near(s).wait_send()


class ColGather:
    def __init__(self, at, block, send, recv):
        self.at, self.block, self.send, self.recv = at, block, send, recv

    def hop(self, way, t):
        at = self.at
        step = 1 if way == 0 else -1
        block = self.block(at.c - step * t)
        return copy(block, block, self.send.at[way, t], self.recv.at[way, t + 1], (at.r, at.c + step))

    def hop_in(self, way, t):
        at = self.at
        step = 1 if way == 0 else -1
        block = self.block(at.c - step * t)
        return copy(block, block, self.send.at[way, t], self.recv.at[way, t], (at.r, at.c - step))

    def has(self, way, t):
        return self.at.c >= t if way == 0 else self.at.c < self.at.cols_n - t

    def goes(self, way):
        return self.has(1 - way, 1)

    def start(self):
        for way in range(2):
            pl.when(self.goes(way))(self.hop(way, 0).start)

    def take(self, t, use=None):
        for way in range(2):

            @pl.when(self.has(way, t))
            def _(way=way):
                self.hop_in(way, t).wait_recv()
                if t + 1 < self.at.cols_n:
                    pl.when(self.goes(way))(self.hop(way, t).start)
                if use is not None:
                    use(self.at.c - t if way == 0 else self.at.c + t)

    def finish(self):
        for way in range(2):
            for t in range(self.at.cols_n - 1):
                pl.when(self.has(way, t) & self.goes(way))(self.hop(way, t).wait_send)


def update_kernel(
    rows_n, cols_n, left_ref, gram_ref, solved_ref, right_ref, d_ref, rows_ref, reduced_ref,
    chosen, solved, mine, top_out, top_in, low_out, low_in, low_all,
    c_send, c_recv, cs_send, cs_recv, v_send, v_recv, vs_send, vs_recv,
    t_send, t_recv, l_send, l_recv, z_send, z_recv, y_send, y_recv, m_send, m_recv,
    d_send, d_recv, ds_send, ds_recv,
):
    at = Place(rows_n, cols_n)
    r, c, chips = at.r, at.c, at.chips
    b, w = right_ref.shape[0], low_all.shape[2]
    deep = solved_ref.shape[0]

    barrier = pltpu.get_barrier_semaphore()
    for s in range(1, chips):
        pl.semaphore_signal(barrier, inc=1, device_id=at.peer(s), device_id_type=MESH)
    for u in range(1, cols_n):
        pl.semaphore_signal(barrier, inc=1, device_id=(r, (c + u) % cols_n), device_id_type=MESH)
    pl.semaphore_signal(barrier, inc=1, device_id=at.sibling, device_id_type=MESH)
    pl.semaphore_wait(barrier, chips + cols_n - 1)

    def span(q, size):
        return pl.ds(pl.multiple_of(q * size, size), size)

    def sems(*refs):
        return [lambda s, ref=ref: ref.at[s] for ref in refs]

    def to_owner(q, out, into, send, recv):
        return copy(out.at[q], into.at[c], send.at[q], recv.at[c], (r, q))

    def from_owner(q, out, into, send, recv):
        return copy(out.at[q], into.at[q], send.at[q], recv.at[q], (r, q))

    def product(rows, q):
        return lax.dot_general(
            rows, chosen[span(q, w), :], (((1,), (1,)), ((), ())), preferred_element_type=jnp.float32
        )

    def total(start, out, into, pair):
        value = start - out[c]
        for u in range(1, cols_n):
            q = (c + u) % cols_n
            from_owner(q, out, into, *pair).wait_recv()
            value = value - into[q]
        return value

    def piece(q):
        return RowGather(
            at, d_ref.at[q, span(r, b)], lambda i: d_ref.at[q, span(i, b)],
            *[lambda s, ref=ref: ref.at[q, s] for ref in (d_send, d_recv, ds_send, ds_recv)]
        )

    def pieces(t, act):
        if t == 0:
            act(piece(c))
        else:
            pl.when(c >= t)(lambda: act(piece(c - t)))
            pl.when(c < cols_n - t)(lambda: act(piece(c + t)))

    top_sems, low_sems = (t_send, t_recv), (l_send, l_recv)
    first = RowGather(
        at, left_ref.at[pl.ds(0, b)], lambda i: chosen.at[span(i, b)], *sems(c_send, c_recv, cs_send, cs_recv)
    )
    second = RowGather(
        at, solved_ref, lambda i: solved.at[span(i, deep)], *sems(v_send, v_recv, vs_send, vs_recv)
    )

    def sent(s):
        first.near_in(s).wait_recv()
        q = at.origin(s)
        top_out[q] = product(left_ref[:b], q)
        pl.when(q != c)(lambda: to_owner(q, top_out, top_in, *top_sems).start())

    first.start()
    chosen[span(r, b), :] = left_ref[:b]
    for s in range(chips):
        first.relay(s)
        if s != 1:
            sent(max(s - 1, 0))
    second.start()
    sent(chips - 1)
    mine[c] = left_ref[:b]
    solved[span(r, deep), :] = solved_ref[...]
    for s in range(chips):
        low_out[at.origin(s)] = product(left_ref[b:], at.origin(s))

    across = ColGather(at, lambda q: d_ref.at[q, span(r, b)], z_send, z_recv)
    others = ColGather(at, lambda q: mine.at[q], m_send, m_recv)
    lows = ColGather(at, lambda q: low_all.at[q], y_send, y_recv)
    d_ref[c, span(r, b), :] = total(gram_ref[:b], top_out, top_in, top_sems)
    across.start()
    piece(c).start()
    for u in range(1, cols_n):
        to_owner((c + u) % cols_n, low_out, low_in, *low_sems).start()
    for t in range(1, cols_n):
        across.take(t, lambda q: piece(q).start())
        if t == 1:
            others.start()
        pieces(t - 1, lambda part: part.relay_all())
    low_all[c] = total(gram_ref[b:], low_out, low_in, low_sems)
    lows.start()
    for t in range(1, cols_n):
        others.take(t)
        second.relay(t)
        lows.take(t)
    pieces(cols_n - 1, lambda part: part.relay_all())
    second.arrive()
    for q in range(cols_n):
        rows_ref[:b, q * w : (q + 1) * w] = d_ref[q, span(r, b), :]
        rows_ref[b:, q * w : (q + 1) * w] = low_all[q]
    value = right_ref[...]
    for i in range(rows_n):
        half = i % at.pair
        value = value - jnp.dot(
            mine[i // at.pair, :, half * deep : (half + 1) * deep],
            solved[i * deep : (i + 1) * deep, :],
            preferred_element_type=jnp.float32,
        )
    reduced_ref[...] = value
    for t in range(cols_n):
        pieces(t, lambda part: part.arrive())
    for t in range(cols_n):
        pieces(t, lambda part: part.finish())
    first.finish()
    second.finish()
    across.finish()
    others.finish()
    lows.finish()
    for u in range(1, cols_n):
        q = (c + u) % cols_n
        to_owner(q, top_out, top_in, *top_sems).wait_send()
        to_owner(q, low_out, low_in, *low_sems).wait_send()


def updated(left_factor, gram_panel, solved_prev, right_block):
    rows_n, cols_n = lax.axis_size("row"), lax.axis_size("col")
    rows, w = gram_panel.shape
    b, wide = right_block.shape
    size = rows_n * b
    f32, bf16 = jnp.float32, jnp.bfloat16
    vmem = pl.BlockSpec(memory_space=pltpu.VMEM)
    line = pltpu.SemaphoreType.DMA((cols_n,))
    ways = pltpu.SemaphoreType.DMA((2, cols_n))
    square = pltpu.SemaphoreType.DMA((cols_n, cols_n))
    return pl.pallas_call(
        functools.partial(update_kernel, rows_n, cols_n),
        out_shape=(
            jax.ShapeDtypeStruct((cols_n, size, w), f32),
            jax.ShapeDtypeStruct((rows, size), f32),
            jax.ShapeDtypeStruct((b, wide), f32),
        ),
        in_specs=[vmem] * 4,
        out_specs=(vmem,) * 3,
        scratch_shapes=[
            pltpu.VMEM((size, left_factor.shape[1]), bf16),
            pltpu.VMEM((rows_n * solved_prev.shape[0], wide), bf16),
            pltpu.VMEM((cols_n, b, left_factor.shape[1]), bf16),
        ]
        + [pltpu.VMEM((cols_n, b, w), f32)] * 2
        + [pltpu.VMEM((cols_n, rows - b, w), f32)] * 3
        + [line] * 12
        + [ways] * 6
        + [square] * 4,
        compiler_params=pltpu.CompilerParams(
            collective_id=0, has_side_effects=True, vmem_limit_bytes=52 * 1024 * 1024
        ),
        cost_estimate=pl.CostEstimate(flops=2 * size * rows * 1024, bytes_accessed=192 * size * size, transcendentals=0),
    )(left_factor, gram_panel, solved_prev, right_block)


def body(gram_panel, left_factor, solved_prev, right_block):
    row_place = lax.axis_index("row")
    col_place = lax.axis_index("col")
    b = right_block.shape[0]
    w = gram_panel.shape[1]
    diagonal, update, reduced = updated(left_factor, gram_panel, solved_prev, right_block)
    reduced = lax.all_gather(reduced, "row", axis=0, tiled=True)
    inverse = invert(diagonal)
    panel_factor = lax.dot_general(
        update,
        lax.dynamic_slice_in_dim(inverse, col_place * w, w, 0),
        (((1,), (1,)), ((), ())),
        precision=lax.Precision.HIGH,
    )
    solved_panel = jnp.dot(
        lax.dynamic_slice_in_dim(inverse, row_place * b, b, 0),
        reduced,
        precision=lax.Precision.HIGH,
    )
    return (panel_factor, solved_panel)


def solution(mesh):
    in_specs = (P("row", "col"), P("row", "col"), P("row", "col"), P("row", "col"))
    out_specs = (P("row", "col"), P("row", "col"))
    return jax.shard_map(body, mesh=mesh, in_specs=in_specs, out_specs=out_specs, check_vma=False)
```

```python
import functools

import jax
import jax.numpy as jnp
from jax import lax
from jax.experimental import pallas as pl
from jax.experimental.pallas import tpu as pltpu
from jax.sharding import PartitionSpec as P

STRIP = 8
TILE = 128
TALL = 256


def halves(value):
    high = value.astype(jnp.bfloat16)
    low = (value - high.astype(jnp.float32)).astype(jnp.bfloat16)
    return high, low


def dot3(left, right, dims=((1,), (0,))):
    lh, ll = halves(left)
    rh, rl = halves(right)
    a = jnp.concatenate([lh, lh, ll], axis=dims[0][0])
    b = jnp.concatenate([rh, rl, rh], axis=dims[1][0])
    return lax.dot_general(a, b, (dims, ((), ())), preferred_element_type=jnp.float32)


def reciprocal(value):
    guess = pl.reciprocal(value, approx=True)
    return guess * (2.0 - value * guess)


def spread_row(value, j):
    return jnp.broadcast_to(value[j : j + 1], (STRIP, TILE))


def spread_lane(value, k):
    return jnp.broadcast_to(value[:, k : k + 1], (STRIP, TILE))


def invert_tile(a):
    lane = lax.broadcasted_iota(jnp.int32, (STRIP, TILE), 1)
    sub = lax.broadcasted_iota(jnp.int32, (STRIP, TILE), 0)
    lane_all = lax.broadcasted_iota(jnp.int32, (TILE, TILE), 1)
    done = []
    strip, below = a[:STRIP], a[STRIP:]
    for g in range(TILE // STRIP):
        lo = g * STRIP
        hi = lo + STRIP
        cols = [spread_lane(strip, lo + k) for k in range(STRIP)]
        t = jnp.where((lane >= lo) & (lane < hi), (lane - lo == sub).astype(jnp.float32), strip)
        out = jnp.zeros_like(t)
        for j in range(0, STRIP, 2):
            p11, p12, p22 = spread_row(cols[j], j), spread_row(cols[j + 1], j), spread_row(cols[j + 1], j + 1)
            det = p11 * p22 - p12 * p12
            inv = reciprocal(det)
            row1, row2 = spread_row(t, j), spread_row(t, j + 1)
            root = lax.rsqrt(p11)
            out = jnp.where(sub == j, row1 * root, out)
            out = jnp.where(sub == j + 1, (row2 * p11 - row1 * p12) * (root * lax.rsqrt(det)), out)
            one = (cols[j] * p22 - cols[j + 1] * p12) * inv
            two = (cols[j + 1] * p11 - cols[j] * p12) * inv
            cross = p12 * inv
            one = jnp.where(sub == j, 1.0 - p22 * inv, jnp.where(sub == j + 1, cross, one))
            two = jnp.where(sub == j, cross, jnp.where(sub == j + 1, 1.0 - p11 * inv, two))
            t = t - one * row1 - two * row2
            for k in range(j + 2, STRIP):
                cols[k] = cols[k] - one * spread_row(cols[k], j) - two * spread_row(cols[k], j + 1)
        done.append(jnp.where(lane < hi, out, 0.0))
        if hi < TILE:
            sent = strip.T[hi:]
            strip = jnp.where((lane >= lo) & (lane < hi), 0.0, below[:STRIP])
            for k in range(STRIP):
                strip = strip - spread_lane(sent[:STRIP], k) * spread_row(t, k)
            if hi + STRIP < TILE:
                inside = lane_all[: TILE - hi - STRIP]
                inside = (inside >= lo) & (inside < hi)
                below = jnp.where(inside, 0.0, below[STRIP:]) - dot3(sent[STRIP:], t)
    return jnp.concatenate(done, axis=0)


def travels(q, j, count):
    gap = (j + count - q) % count
    return (2 * gap < count) | ((2 * gap == count) & (2 * q < count))


def inverse_kernel(d_ref, o_ref, w_ref):
    pieces, size, width = d_ref.shape
    count = size // TILE
    for q in range(pieces):
        rows = slice(q * width, (q + 1) * width)
        for j in range(q, pieces):
            block = d_ref[j, rows, :] if travels(q, j, pieces) else d_ref[q, j * width : (j + 1) * width, :].T
            w_ref[rows, j * width : (j + 1) * width] = block
    lane = lax.broadcasted_iota(jnp.int32, (TILE, size), 1)
    eye = (
        lax.broadcasted_iota(jnp.int32, (TILE, TILE), 0)
        == lax.broadcasted_iota(jnp.int32, (TILE, TILE), 1)
    ).astype(jnp.float32)
    across, down = [], []
    for i in range(count):
        tile = slice(i * TILE, (i + 1) * TILE)
        only = jnp.where(eye > 0, w_ref[tile, tile], 0.0)
        across.append(lax.rsqrt(jnp.sum(only, axis=0, keepdims=True)))
        down.append(lax.rsqrt(jnp.sum(only, axis=1, keepdims=True)))
    scale = jnp.concatenate(across, axis=1)
    for i in range(count):
        tile = slice(i * TILE, (i + 1) * TILE)
        w_ref[tile, i * TILE :] = w_ref[tile, i * TILE :] * down[i] * scale[:, i * TILE :]

    def step(k, carry):
        at = pl.multiple_of(k * TILE, TILE)
        here = pl.ds(at, TILE)
        small = invert_tile(w_ref[here, here])
        w_ref[here, here] = eye
        z = dot3(small, w_ref[here, :])
        o_ref[here, :] = jnp.where(lane < at + TILE, z * scale, 0.0)
        w_ref[here, :] = z
        zh, zl = halves(z)
        right = jnp.concatenate([zh, zl, zh], axis=0)

        def trail(i, c):
            start = pl.multiple_of(i * TALL, TALL)
            mine = pl.ds(start, TALL)
            later = start + lax.broadcasted_iota(jnp.int32, (TALL, TILE), 0) >= at + TILE
            yh, yl = halves(jnp.where(later, w_ref[here, mine].T, 0.0))
            left = jnp.concatenate([yh, yh, yl], axis=1)
            w_ref[mine, here] = jnp.where(later, 0.0, w_ref[mine, here])
            w_ref[mine, :] -= jnp.dot(left, right, preferred_element_type=jnp.float32)
            return c

        lax.fori_loop((k + 1) // (TALL // TILE), size // TALL, trail, 0)
        return carry

    lax.fori_loop(0, count, step, 0)


def invert(diagonal):
    size = diagonal.shape[1]
    return pl.pallas_call(
        inverse_kernel,
        out_shape=jax.ShapeDtypeStruct((size, size), jnp.float32),
        in_specs=[pl.BlockSpec(memory_space=pltpu.VMEM)],
        out_specs=pl.BlockSpec(memory_space=pltpu.VMEM),
        scratch_shapes=[pltpu.VMEM((size, size), jnp.float32)],
        compiler_params=pltpu.CompilerParams(vmem_limit_bytes=40 * 1024 * 1024),
        cost_estimate=pl.CostEstimate(flops=4 * size**3, bytes_accessed=192 * size * size, transcendentals=0),
    )(diagonal)


MESH = pl.DeviceIdType.MESH


def copy(src, dst, send, recv, to):
    return pltpu.make_async_remote_copy(
        src_ref=src, dst_ref=dst, send_sem=send, recv_sem=recv, device_id=to, device_id_type=MESH
    )


class Place:
    def __init__(self, rows_n, cols_n):
        self.cols_n = cols_n
        self.pair = rows_n // cols_n
        self.chips = rows_n // self.pair
        self.r = lax.axis_index("row")
        self.c = lax.axis_index("col")
        self.core = self.r % self.pair
        self.p = self.r // self.pair
        self.sibling = (self.p * self.pair + (self.pair - 1 - self.core), self.c)

    def peer(self, s):
        return (((self.p + s) % self.chips) * self.pair + self.core, self.c)

    def origin(self, s):
        return (self.p + self.chips - s) % self.chips


class RowGather:
    def __init__(self, at, own, block, send, recv, side_send, side_recv, wanted=None):
        self.at, self.own, self.block, self.wanted = at, own, block, wanted
        self.send, self.recv, self.side_send, self.side_recv = send, recv, side_send, side_recv

    def when(self, s, act):
        if self.wanted is None:
            act()
        else:
            pl.when(self.wanted(self.at.origin(s)))(act)

    def far(self, s):
        at = self.at
        return copy(self.own, self.block(at.r), self.send(s), self.recv(s), at.peer(s))

    def far_in(self, s):
        at = self.at
        block = self.block(at.origin(s) * at.pair + at.core)
        return copy(block, block, self.send(s), self.recv(s), at.peer(s))

    def near(self, s):
        at = self.at
        block = self.block(at.origin(s) * at.pair + at.core)
        src = self.own if s == 0 else block
        return copy(src, block, self.side_send(s), self.side_recv(s), at.sibling)

    def near_in(self, s):
        at = self.at
        block = self.block(at.origin(s) * at.pair + (at.pair - 1 - at.core))
        return copy(block, block, self.side_send(s), self.side_recv(s), at.sibling)

    def start(self):
        def act():
            for s in range(1, self.at.chips):
                self.far(s).start()
            self.near(0).start()

        self.when(0, act)

    def relay(self, s):
        def act():
            self.far_in(s).wait_recv()
            self.near(s).start()

        if s > 0:
            self.when(s, act)

    def relay_all(self):
        for s in range(1, self.at.chips):
            self.relay(s)

    def arrive(self):
        for s in range(self.at.chips):
            self.when(s, lambda s=s: self.near_in(s).wait_recv())

    def finish(self):
        def act():
            for s in range(1, self.at.chips):
                self.far(s).wait_send()

        self.when(0, act)
        for s in range(self.at.chips):
            self.when(s, lambda s=s: self.near(s).wait_send())


class ColGather:
    def __init__(self, at, block, send, recv):
        self.at, self.block, self.send, self.recv = at, block, send, recv

    def hop(self, way, t):
        at = self.at
        step = 1 if way == 0 else -1
        block = self.block(at.c - step * t)
        return copy(block, block, self.send.at[way, t], self.recv.at[way, t + 1], (at.r, at.c + step))

    def hop_in(self, way, t):
        at = self.at
        step = 1 if way == 0 else -1
        block = self.block(at.c - step * t)
        return copy(block, block, self.send.at[way, t], self.recv.at[way, t], (at.r, at.c - step))

    def has(self, way, t):
        return self.at.c >= t if way == 0 else self.at.c < self.at.cols_n - t

    def goes(self, way):
        return self.has(1 - way, 1)

    def start(self):
        for way in range(2):
            pl.when(self.goes(way))(self.hop(way, 0).start)

    def take(self, t, use=None):
        for way in range(2):

            @pl.when(self.has(way, t))
            def _(way=way):
                self.hop_in(way, t).wait_recv()
                if t + 1 < self.at.cols_n:
                    pl.when(self.goes(way))(self.hop(way, t).start)
                if use is not None:
                    use(self.at.c - t if way == 0 else self.at.c + t)

    def finish(self):
        for way in range(2):
            for t in range(self.at.cols_n - 1):
                pl.when(self.has(way, t) & self.goes(way))(self.hop(way, t).wait_send)


def update_kernel(
    rows_n, cols_n, left_ref, gram_ref, solved_ref, right_ref, d_ref, rows_ref, reduced_ref,
    chosen, solved, mine, top_out, top_in, low_out, low_in, low_all,
    c_send, c_recv, cs_send, cs_recv, v_send, v_recv, vs_send, vs_recv,
    t_send, t_recv, l_send, l_recv, z_send, z_recv, y_send, y_recv, m_send, m_recv,
    d_send, d_recv, ds_send, ds_recv,
):
    at = Place(rows_n, cols_n)
    r, c, chips = at.r, at.c, at.chips
    b, w = right_ref.shape[0], low_all.shape[2]
    deep = solved_ref.shape[0]

    barrier = pltpu.get_barrier_semaphore()
    for s in range(1, chips):
        pl.semaphore_signal(barrier, inc=1, device_id=at.peer(s), device_id_type=MESH)
    for u in range(1, cols_n):
        pl.semaphore_signal(barrier, inc=1, device_id=(r, (c + u) % cols_n), device_id_type=MESH)
    pl.semaphore_signal(barrier, inc=1, device_id=at.sibling, device_id_type=MESH)
    pl.semaphore_wait(barrier, chips + cols_n - 1)

    def span(q, size):
        return pl.ds(pl.multiple_of(q * size, size), size)

    def sems(*refs):
        return [lambda s, ref=ref: ref.at[s] for ref in refs]

    def to_owner(q, out, into, send, recv):
        return copy(out.at[q], into.at[c], send.at[q], recv.at[c], (r, q))

    def from_owner(q, out, into, send, recv):
        return copy(out.at[q], into.at[q], send.at[q], recv.at[q], (r, q))

    def product(rows, q):
        return lax.dot_general(
            rows, chosen[span(q, w), :], (((1,), (1,)), ((), ())), preferred_element_type=jnp.float32
        )

    def total(start, out, into, pair):
        value = start - out[c]
        for u in range(1, cols_n):
            q = (c + u) % cols_n
            from_owner(q, out, into, *pair).wait_recv()
            value = value - into[q]
        return value

    def piece(q):
        return RowGather(
            at, d_ref.at[q, span(r, b)], lambda i: d_ref.at[q, span(i, b)],
            *[lambda s, ref=ref: ref.at[q, s] for ref in (d_send, d_recv, ds_send, ds_recv)],
            wanted=lambda i: travels(i, q, cols_n),
        )

    def pieces(t, act):
        if t == 0:
            act(piece(c))
        else:
            pl.when(c >= t)(lambda: act(piece(c - t)))
            pl.when(c < cols_n - t)(lambda: act(piece(c + t)))

    top_sems, low_sems = (t_send, t_recv), (l_send, l_recv)
    first = RowGather(
        at, left_ref.at[pl.ds(0, b)], lambda i: chosen.at[span(i, b)], *sems(c_send, c_recv, cs_send, cs_recv)
    )
    second = RowGather(
        at, solved_ref, lambda i: solved.at[span(i, deep)], *sems(v_send, v_recv, vs_send, vs_recv)
    )

    def sent(s):
        first.near_in(s).wait_recv()
        q = at.origin(s)
        top_out[q] = product(left_ref[:b], q)
        pl.when(q != c)(lambda: to_owner(q, top_out, top_in, *top_sems).start())

    first.start()
    chosen[span(r, b), :] = left_ref[:b]
    for s in range(chips):
        first.relay(s)
        if s != 1:
            sent(max(s - 1, 0))
    second.start()
    sent(chips - 1)
    mine[c] = left_ref[:b]
    solved[span(r, deep), :] = solved_ref[...]
    for s in range(chips):
        low_out[at.origin(s)] = product(left_ref[b:], at.origin(s))

    across = ColGather(at, lambda q: d_ref.at[q, span(r, b)], z_send, z_recv)
    others = ColGather(at, lambda q: mine.at[q], m_send, m_recv)
    lows = ColGather(at, lambda q: low_all.at[q], y_send, y_recv)
    d_ref[c, span(r, b), :] = total(gram_ref[:b], top_out, top_in, top_sems)
    across.start()
    piece(c).start()
    for u in range(1, cols_n):
        to_owner((c + u) % cols_n, low_out, low_in, *low_sems).start()
    for t in range(1, cols_n):
        across.take(t, lambda q: piece(q).start())
        if t == 1:
            others.start()
        pieces(t - 1, lambda part: part.relay_all())
    low_all[c] = total(gram_ref[b:], low_out, low_in, low_sems)
    lows.start()
    for t in range(1, cols_n):
        others.take(t)
        second.relay(t)
        lows.take(t)
    pieces(cols_n - 1, lambda part: part.relay_all())
    second.arrive()
    for q in range(cols_n):
        rows_ref[:b, q * w : (q + 1) * w] = d_ref[q, span(r, b), :]
        rows_ref[b:, q * w : (q + 1) * w] = low_all[q]
    value = right_ref[...]
    for i in range(rows_n):
        half = i % at.pair
        value = value - jnp.dot(
            mine[i // at.pair, :, half * deep : (half + 1) * deep],
            solved[i * deep : (i + 1) * deep, :],
            preferred_element_type=jnp.float32,
        )
    reduced_ref[...] = value
    for t in range(cols_n):
        pieces(t, lambda part: part.arrive())
    for t in range(cols_n):
        pieces(t, lambda part: part.finish())
    first.finish()
    second.finish()
    across.finish()
    others.finish()
    lows.finish()
    for u in range(1, cols_n):
        q = (c + u) % cols_n
        to_owner(q, top_out, top_in, *top_sems).wait_send()
        to_owner(q, low_out, low_in, *low_sems).wait_send()


def updated(left_factor, gram_panel, solved_prev, right_block):
    rows_n, cols_n = lax.axis_size("row"), lax.axis_size("col")
    rows, w = gram_panel.shape
    b, wide = right_block.shape
    size = rows_n * b
    f32, bf16 = jnp.float32, jnp.bfloat16
    vmem = pl.BlockSpec(memory_space=pltpu.VMEM)
    line = pltpu.SemaphoreType.DMA((cols_n,))
    ways = pltpu.SemaphoreType.DMA((2, cols_n))
    square = pltpu.SemaphoreType.DMA((cols_n, cols_n))
    return pl.pallas_call(
        functools.partial(update_kernel, rows_n, cols_n),
        out_shape=(
            jax.ShapeDtypeStruct((cols_n, size, w), f32),
            jax.ShapeDtypeStruct((rows, size), f32),
            jax.ShapeDtypeStruct((b, wide), f32),
        ),
        in_specs=[vmem] * 4,
        out_specs=(vmem,) * 3,
        scratch_shapes=[
            pltpu.VMEM((size, left_factor.shape[1]), bf16),
            pltpu.VMEM((rows_n * solved_prev.shape[0], wide), bf16),
            pltpu.VMEM((cols_n, b, left_factor.shape[1]), bf16),
        ]
        + [pltpu.VMEM((cols_n, b, w), f32)] * 2
        + [pltpu.VMEM((cols_n, rows - b, w), f32)] * 3
        + [line] * 12
        + [ways] * 6
        + [square] * 4,
        compiler_params=pltpu.CompilerParams(
            collective_id=0, has_side_effects=True, vmem_limit_bytes=52 * 1024 * 1024
        ),
        cost_estimate=pl.CostEstimate(flops=2 * size * rows * 1024, bytes_accessed=192 * size * size, transcendentals=0),
    )(left_factor, gram_panel, solved_prev, right_block)


def body(gram_panel, left_factor, solved_prev, right_block):
    row_place = lax.axis_index("row")
    col_place = lax.axis_index("col")
    b = right_block.shape[0]
    w = gram_panel.shape[1]
    diagonal, update, reduced = updated(left_factor, gram_panel, solved_prev, right_block)
    reduced = lax.all_gather(reduced, "row", axis=0, tiled=True)
    inverse = invert(diagonal)
    panel_factor = lax.dot_general(
        update,
        lax.dynamic_slice_in_dim(inverse, col_place * w, w, 0),
        (((1,), (1,)), ((), ())),
        precision=lax.Precision.HIGH,
    )
    solved_panel = jnp.dot(
        lax.dynamic_slice_in_dim(inverse, row_place * b, b, 0),
        reduced,
        precision=lax.Precision.HIGH,
    )
    return (panel_factor, solved_panel)


def solution(mesh):
    in_specs = (P("row", "col"), P("row", "col"), P("row", "col"), P("row", "col"))
    out_specs = (P("row", "col"), P("row", "col"))
    return jax.shard_map(body, mesh=mesh, in_specs=in_specs, out_specs=out_specs, check_vma=False)
```

```python
import functools

import jax
import jax.numpy as jnp
from jax import lax
from jax.experimental import pallas as pl
from jax.experimental.pallas import tpu as pltpu
from jax.sharding import PartitionSpec as P

STRIP = 8
TILE = 128
TALL = 256


def halves(value):
    high = value.astype(jnp.bfloat16)
    low = (value - high.astype(jnp.float32)).astype(jnp.bfloat16)
    return high, low


def dot3(left, right, dims=((1,), (0,))):
    lh, ll = halves(left)
    rh, rl = halves(right)
    a = jnp.concatenate([lh, lh, ll], axis=dims[0][0])
    b = jnp.concatenate([rh, rl, rh], axis=dims[1][0])
    return lax.dot_general(a, b, (dims, ((), ())), preferred_element_type=jnp.float32)


def reciprocal(value):
    guess = pl.reciprocal(value, approx=True)
    return guess * (2.0 - value * guess)


def spread_row(value, j):
    return jnp.broadcast_to(value[j : j + 1], (STRIP, TILE))


def spread_lane(value, k):
    return jnp.broadcast_to(value[:, k : k + 1], (STRIP, TILE))


def invert_tile(a):
    lane = lax.broadcasted_iota(jnp.int32, (STRIP, TILE), 1)
    sub = lax.broadcasted_iota(jnp.int32, (STRIP, TILE), 0)
    lane_all = lax.broadcasted_iota(jnp.int32, (TILE, TILE), 1)
    done = []
    strip, below = a[:STRIP], a[STRIP:]
    for g in range(TILE // STRIP):
        lo = g * STRIP
        hi = lo + STRIP
        cols = [spread_lane(strip, lo + k) for k in range(STRIP)]
        t = jnp.where((lane >= lo) & (lane < hi), (lane - lo == sub).astype(jnp.float32), strip)
        out = jnp.zeros_like(t)
        for j in range(0, STRIP, 2):
            p11, p12, p22 = spread_row(cols[j], j), spread_row(cols[j + 1], j), spread_row(cols[j + 1], j + 1)
            det = p11 * p22 - p12 * p12
            inv = reciprocal(det)
            row1, row2 = spread_row(t, j), spread_row(t, j + 1)
            root = lax.rsqrt(p11)
            out = jnp.where(sub == j, row1 * root, out)
            out = jnp.where(sub == j + 1, (row2 * p11 - row1 * p12) * (root * lax.rsqrt(det)), out)
            one = (cols[j] * p22 - cols[j + 1] * p12) * inv
            two = (cols[j + 1] * p11 - cols[j] * p12) * inv
            cross = p12 * inv
            one = jnp.where(sub == j, 1.0 - p22 * inv, jnp.where(sub == j + 1, cross, one))
            two = jnp.where(sub == j, cross, jnp.where(sub == j + 1, 1.0 - p11 * inv, two))
            t = t - one * row1 - two * row2
            for k in range(j + 2, STRIP):
                cols[k] = cols[k] - one * spread_row(cols[k], j) - two * spread_row(cols[k], j + 1)
        done.append(jnp.where(lane < hi, out, 0.0))
        if hi < TILE:
            sent = strip.T[hi:]
            strip = jnp.where((lane >= lo) & (lane < hi), 0.0, below[:STRIP])
            for k in range(STRIP):
                strip = strip - spread_lane(sent[:STRIP], k) * spread_row(t, k)
            if hi + STRIP < TILE:
                inside = lane_all[: TILE - hi - STRIP]
                inside = (inside >= lo) & (inside < hi)
                below = jnp.where(inside, 0.0, below[STRIP:]) - dot3(sent[STRIP:], t)
    return jnp.concatenate(done, axis=0)


def travels(q, j, count):
    gap = (j + count - q) % count
    return (2 * gap < count) | ((2 * gap == count) & (2 * q < count))


def inverse_kernel(d_ref, o_ref, w_ref):
    pieces, size, width = d_ref.shape
    count = size // TILE
    for q in range(pieces):
        rows = slice(q * width, (q + 1) * width)
        for j in range(q, pieces):
            block = d_ref[j, rows, :] if travels(q, j, pieces) else d_ref[q, j * width : (j + 1) * width, :].T
            w_ref[rows, j * width : (j + 1) * width] = block
    lane = lax.broadcasted_iota(jnp.int32, (TILE, size), 1)
    eye = (
        lax.broadcasted_iota(jnp.int32, (TILE, TILE), 0)
        == lax.broadcasted_iota(jnp.int32, (TILE, TILE), 1)
    ).astype(jnp.float32)
    across, down = [], []
    for i in range(count):
        tile = slice(i * TILE, (i + 1) * TILE)
        only = jnp.where(eye > 0, w_ref[tile, tile], 0.0)
        across.append(lax.rsqrt(jnp.sum(only, axis=0, keepdims=True)))
        down.append(lax.rsqrt(jnp.sum(only, axis=1, keepdims=True)))
    scale = jnp.concatenate(across, axis=1)
    for i in range(count):
        tile = slice(i * TILE, (i + 1) * TILE)
        w_ref[tile, i * TILE :] = w_ref[tile, i * TILE :] * down[i] * scale[:, i * TILE :]

    def step(k, carry):
        at = pl.multiple_of(k * TILE, TILE)
        here = pl.ds(at, TILE)
        small = invert_tile(w_ref[here, here])
        w_ref[here, here] = eye
        z = dot3(small, w_ref[here, :])
        o_ref[here, :] = jnp.where(lane < at + TILE, z * scale, 0.0)
        w_ref[here, :] = z
        zh, zl = halves(z)
        right = jnp.concatenate([zh, zl, zh], axis=0)

        def trail(i, c):
            start = pl.multiple_of(i * TALL, TALL)
            mine = pl.ds(start, TALL)
            later = start + lax.broadcasted_iota(jnp.int32, (TALL, TILE), 0) >= at + TILE
            yh, yl = halves(jnp.where(later, w_ref[here, mine].T, 0.0))
            left = jnp.concatenate([yh, yh, yl], axis=1)
            w_ref[mine, here] = jnp.where(later, 0.0, w_ref[mine, here])
            w_ref[mine, :] -= jnp.dot(left, right, preferred_element_type=jnp.float32)
            return c

        lax.fori_loop((k + 1) // (TALL // TILE), size // TALL, trail, 0)
        return carry

    lax.fori_loop(0, count, step, 0)


def invert(diagonal):
    size = diagonal.shape[1]
    return pl.pallas_call(
        inverse_kernel,
        out_shape=jax.ShapeDtypeStruct((size, size), jnp.float32),
        in_specs=[pl.BlockSpec(memory_space=pltpu.VMEM)],
        out_specs=pl.BlockSpec(memory_space=pltpu.VMEM),
        scratch_shapes=[pltpu.VMEM((size, size), jnp.float32)],
        compiler_params=pltpu.CompilerParams(vmem_limit_bytes=40 * 1024 * 1024),
        cost_estimate=pl.CostEstimate(flops=4 * size**3, bytes_accessed=192 * size * size, transcendentals=0),
    )(diagonal)


MESH = pl.DeviceIdType.MESH


def copy(src, dst, send, recv, to):
    return pltpu.make_async_remote_copy(
        src_ref=src, dst_ref=dst, send_sem=send, recv_sem=recv, device_id=to, device_id_type=MESH
    )


class Place:
    def __init__(self, rows_n, cols_n):
        self.cols_n = cols_n
        self.pair = rows_n // cols_n
        self.chips = rows_n // self.pair
        self.r = lax.axis_index("row")
        self.c = lax.axis_index("col")
        self.core = self.r % self.pair
        self.p = self.r // self.pair
        self.sibling = (self.p * self.pair + (self.pair - 1 - self.core), self.c)

    def peer(self, s):
        return (((self.p + s) % self.chips) * self.pair + self.core, self.c)

    def origin(self, s):
        return (self.p + self.chips - s) % self.chips


class RowGather:
    def __init__(self, at, own, block, send, recv, side_send, side_recv, wanted=None):
        self.at, self.own, self.block, self.wanted = at, own, block, wanted
        self.send, self.recv, self.side_send, self.side_recv = send, recv, side_send, side_recv

    def when(self, s, act):
        if self.wanted is None:
            act()
        else:
            pl.when(self.wanted(self.at.origin(s)))(act)

    def far(self, s):
        at = self.at
        return copy(self.own, self.block(at.r), self.send(s), self.recv(s), at.peer(s))

    def far_in(self, s):
        at = self.at
        block = self.block(at.origin(s) * at.pair + at.core)
        return copy(block, block, self.send(s), self.recv(s), at.peer(s))

    def near(self, s):
        at = self.at
        block = self.block(at.origin(s) * at.pair + at.core)
        src = self.own if s == 0 else block
        return copy(src, block, self.side_send(s), self.side_recv(s), at.sibling)

    def near_in(self, s):
        at = self.at
        block = self.block(at.origin(s) * at.pair + (at.pair - 1 - at.core))
        return copy(block, block, self.side_send(s), self.side_recv(s), at.sibling)

    def start(self):
        def act():
            for s in range(1, self.at.chips):
                self.far(s).start()
            self.near(0).start()

        self.when(0, act)

    def relay(self, s):
        def act():
            self.far_in(s).wait_recv()
            self.near(s).start()

        if s > 0:
            self.when(s, act)

    def relay_all(self):
        for s in range(1, self.at.chips):
            self.relay(s)

    def arrive(self):
        for s in range(self.at.chips):
            self.when(s, lambda s=s: self.near_in(s).wait_recv())

    def finish(self):
        def act():
            for s in range(1, self.at.chips):
                self.far(s).wait_send()

        self.when(0, act)
        for s in range(self.at.chips):
            self.when(s, lambda s=s: self.near(s).wait_send())


class ColGather:
    def __init__(self, at, block, send, recv):
        self.at, self.block, self.send, self.recv = at, block, send, recv

    def hop(self, way, t):
        at = self.at
        step = 1 if way == 0 else -1
        block = self.block(at.c - step * t)
        return copy(block, block, self.send.at[way, t], self.recv.at[way, t + 1], (at.r, at.c + step))

    def hop_in(self, way, t):
        at = self.at
        step = 1 if way == 0 else -1
        block = self.block(at.c - step * t)
        return copy(block, block, self.send.at[way, t], self.recv.at[way, t], (at.r, at.c - step))

    def has(self, way, t):
        return self.at.c >= t if way == 0 else self.at.c < self.at.cols_n - t

    def goes(self, way):
        return self.has(1 - way, 1)

    def start(self):
        for way in range(2):
            pl.when(self.goes(way))(self.hop(way, 0).start)

    def take(self, t, use=None):
        for way in range(2):

            @pl.when(self.has(way, t))
            def _(way=way):
                self.hop_in(way, t).wait_recv()
                if t + 1 < self.at.cols_n:
                    pl.when(self.goes(way))(self.hop(way, t).start)
                if use is not None:
                    use(self.at.c - t if way == 0 else self.at.c + t)

    def finish(self):
        for way in range(2):
            for t in range(self.at.cols_n - 1):
                pl.when(self.has(way, t) & self.goes(way))(self.hop(way, t).wait_send)


def update_kernel(
    rows_n, cols_n, left_ref, gram_ref, solved_ref, right_ref, d_ref, rows_ref, reduced_ref,
    chosen, solved, mine, top_out, top_in, low_out, low_in, low_all,
    c_send, c_recv, cs_send, cs_recv, v_send, v_recv, vs_send, vs_recv,
    t_send, t_recv, l_send, l_recv, z_send, z_recv, y_send, y_recv, m_send, m_recv,
    d_send, d_recv, ds_send, ds_recv,
):
    at = Place(rows_n, cols_n)
    r, c, chips = at.r, at.c, at.chips
    b, w = right_ref.shape[0], low_all.shape[2]
    deep = solved_ref.shape[0]

    barrier = pltpu.get_barrier_semaphore()
    for s in range(1, chips):
        pl.semaphore_signal(barrier, inc=1, device_id=at.peer(s), device_id_type=MESH)
    for u in range(1, cols_n):
        pl.semaphore_signal(barrier, inc=1, device_id=(r, (c + u) % cols_n), device_id_type=MESH)
    pl.semaphore_signal(barrier, inc=1, device_id=at.sibling, device_id_type=MESH)
    pl.semaphore_wait(barrier, chips + cols_n - 1)

    def span(q, size):
        return pl.ds(pl.multiple_of(q * size, size), size)

    def sems(*refs):
        return [lambda s, ref=ref: ref.at[s] for ref in refs]

    def to_owner(q, out, into, send, recv):
        return copy(out.at[q], into.at[c], send.at[q], recv.at[c], (r, q))

    def from_owner(q, out, into, send, recv):
        return copy(out.at[q], into.at[q], send.at[q], recv.at[q], (r, q))

    def product(rows, q):
        return lax.dot_general(
            rows, chosen[span(q, w), :], (((1,), (1,)), ((), ())), preferred_element_type=jnp.float32
        )

    def total(start, out, into, pair):
        value = start - out[c]
        for u in range(1, cols_n):
            q = (c + u) % cols_n
            from_owner(q, out, into, *pair).wait_recv()
            value = value - into[q]
        return value

    def piece(q):
        return RowGather(
            at, d_ref.at[q, span(r, b)], lambda i: d_ref.at[q, span(i, b)],
            *[lambda s, ref=ref: ref.at[q, s] for ref in (d_send, d_recv, ds_send, ds_recv)],
            wanted=lambda i: travels(i, q, cols_n),
        )

    def pieces(t, act):
        if t == 0:
            act(piece(c))
        else:
            pl.when(c >= t)(lambda: act(piece(c - t)))
            pl.when(c < cols_n - t)(lambda: act(piece(c + t)))

    top_sems, low_sems = (t_send, t_recv), (l_send, l_recv)
    first = RowGather(
        at, left_ref.at[pl.ds(0, b)], lambda i: chosen.at[span(i, b)], *sems(c_send, c_recv, cs_send, cs_recv)
    )
    second = RowGather(
        at, solved_ref, lambda i: solved.at[span(i, deep)], *sems(v_send, v_recv, vs_send, vs_recv)
    )

    def sent(s):
        first.near_in(s).wait_recv()
        q = at.origin(s)
        top_out[q] = product(left_ref[:b], q)
        pl.when(q != c)(lambda: to_owner(q, top_out, top_in, *top_sems).start())

    mine[c] = left_ref[:b]
    others = ColGather(at, lambda q: mine.at[q], m_send, m_recv)
    first.start()
    others.start()
    chosen[span(r, b), :] = left_ref[:b]
    for s in range(chips):
        first.relay(s)
        if s != 1:
            sent(max(s - 1, 0))
    second.start()
    sent(chips - 1)
    others.take(1)
    solved[span(r, deep), :] = solved_ref[...]
    for s in range(chips):
        low_out[at.origin(s)] = product(left_ref[b:], at.origin(s))

    across = ColGather(at, lambda q: d_ref.at[q, span(r, b)], z_send, z_recv)
    lows = ColGather(at, lambda q: low_all.at[q], y_send, y_recv)
    d_ref[c, span(r, b), :] = total(gram_ref[:b], top_out, top_in, top_sems)
    across.start()
    piece(c).start()
    for u in range(1, cols_n):
        to_owner((c + u) % cols_n, low_out, low_in, *low_sems).start()
    for t in range(1, cols_n):
        across.take(t, lambda q: piece(q).start())
        if t > 1:
            others.take(t)
        pieces(t - 1, lambda part: part.relay_all())
    low_all[c] = total(gram_ref[b:], low_out, low_in, low_sems)
    lows.start()
    for t in range(1, cols_n):
        second.relay(t)
        lows.take(t)
    pieces(cols_n - 1, lambda part: part.relay_all())
    second.arrive()
    for q in range(cols_n):
        rows_ref[:b, q * w : (q + 1) * w] = d_ref[q, span(r, b), :]
        rows_ref[b:, q * w : (q + 1) * w] = low_all[q]
    value = right_ref[...]
    for i in range(rows_n):
        half = i % at.pair
        value = value - jnp.dot(
            mine[i // at.pair, :, half * deep : (half + 1) * deep],
            solved[i * deep : (i + 1) * deep, :],
            preferred_element_type=jnp.float32,
        )
    reduced_ref[...] = value
    for t in range(cols_n):
        pieces(t, lambda part: part.arrive())
    for t in range(cols_n):
        pieces(t, lambda part: part.finish())
    first.finish()
    second.finish()
    across.finish()
    others.finish()
    lows.finish()
    for u in range(1, cols_n):
        q = (c + u) % cols_n
        to_owner(q, top_out, top_in, *top_sems).wait_send()
        to_owner(q, low_out, low_in, *low_sems).wait_send()


def updated(left_factor, gram_panel, solved_prev, right_block):
    rows_n, cols_n = lax.axis_size("row"), lax.axis_size("col")
    rows, w = gram_panel.shape
    b, wide = right_block.shape
    size = rows_n * b
    f32, bf16 = jnp.float32, jnp.bfloat16
    vmem = pl.BlockSpec(memory_space=pltpu.VMEM)
    line = pltpu.SemaphoreType.DMA((cols_n,))
    ways = pltpu.SemaphoreType.DMA((2, cols_n))
    square = pltpu.SemaphoreType.DMA((cols_n, cols_n))
    return pl.pallas_call(
        functools.partial(update_kernel, rows_n, cols_n),
        out_shape=(
            jax.ShapeDtypeStruct((cols_n, size, w), f32),
            jax.ShapeDtypeStruct((rows, size), f32),
            jax.ShapeDtypeStruct((b, wide), f32),
        ),
        in_specs=[vmem] * 4,
        out_specs=(vmem,) * 3,
        scratch_shapes=[
            pltpu.VMEM((size, left_factor.shape[1]), bf16),
            pltpu.VMEM((rows_n * solved_prev.shape[0], wide), bf16),
            pltpu.VMEM((cols_n, b, left_factor.shape[1]), bf16),
        ]
        + [pltpu.VMEM((cols_n, b, w), f32)] * 2
        + [pltpu.VMEM((cols_n, rows - b, w), f32)] * 3
        + [line] * 12
        + [ways] * 6
        + [square] * 4,
        compiler_params=pltpu.CompilerParams(
            collective_id=0, has_side_effects=True, vmem_limit_bytes=52 * 1024 * 1024
        ),
        cost_estimate=pl.CostEstimate(flops=2 * size * rows * 1024, bytes_accessed=192 * size * size, transcendentals=0),
    )(left_factor, gram_panel, solved_prev, right_block)


def body(gram_panel, left_factor, solved_prev, right_block):
    row_place = lax.axis_index("row")
    col_place = lax.axis_index("col")
    b = right_block.shape[0]
    w = gram_panel.shape[1]
    diagonal, update, reduced = updated(left_factor, gram_panel, solved_prev, right_block)
    reduced = lax.all_gather(reduced, "row", axis=0, tiled=True)
    inverse = invert(diagonal)
    panel_factor = lax.dot_general(
        update,
        lax.dynamic_slice_in_dim(inverse, col_place * w, w, 0),
        (((1,), (1,)), ((), ())),
        precision=lax.Precision.HIGH,
    )
    solved_panel = jnp.dot(
        lax.dynamic_slice_in_dim(inverse, row_place * b, b, 0),
        reduced,
        precision=lax.Precision.HIGH,
    )
    return (panel_factor, solved_panel)


def solution(mesh):
    in_specs = (P("row", "col"), P("row", "col"), P("row", "col"), P("row", "col"))
    out_specs = (P("row", "col"), P("row", "col"))
    return jax.shard_map(body, mesh=mesh, in_specs=in_specs, out_specs=out_specs, check_vma=False)
```
